128 devices in a mesh: wide: 16 (over x, y), narrow: 8 (over z, core).
Axes of the slice: x: 4, y: 4, z: 4, core: 2. Of those that a mesh axis runs over, the one named last changes fastest.
Arguments:
- queries: bfloat16 [16384, 32, 128], P(('wide', 'narrow')), may hold values from -256 to 256
- keys: bfloat16 [16384, 4, 128], P(('wide', 'narrow')), may hold values from -6 to 6
- values: bfloat16 [16384, 4, 128], P(('wide', 'narrow')), may hold values from -6 to 6
- residual: bfloat16 [16384, 4096], P(('wide', 'narrow')), may hold values from -6 to 6
- out_proj: bfloat16 [4096, 4096], P('narrow'), may hold values from -0.09375 to 0.09375
- norm_gain: float32 [4096], replicated, may hold values from 0.25 to 1.75
- expert_ids: int32 [16384, 8], P(('wide', 'narrow')), may hold values from 0 to 127, all different within a row; in each aligned block of 128 rows (0 to 127, 128 to 255, ...) at most 9 rows name the same one
- gate_weights: float32 [16384, 8], P(('wide', 'narrow')), may hold values from 0.03 to 0.3
- w_gate: bfloat16 [128, 4096, 768], P(('wide', 'narrow')), may hold values from -0.09375 to 0.09375
- w_up: bfloat16 [128, 4096, 768], P(('wide', 'narrow')), may hold values from -0.09375 to 0.09375
- w_down: bfloat16 [128, 768, 4096], P(('wide', 'narrow')), may hold values from -0.21875 to 0.21875
Outputs:
- block_out: bfloat16 [16384, 4096], P(('wide', 'narrow'))
The draws below stay inside these ranges and needn't reach their ends.
Inputs may be any that keep to these rules, and one draw needn't show every extreme that they name: `expert_ids`: in the rows of one device, each expert is named by at most 9 rows; each token names 8 different experts.
All inputs are finite; a program needn't handle non-finite values.
Results may differ from the reference program's by a relative error of at most 0.01.
Values may be sent and summed in bfloat16 or wider, within the bound.
A program may use at most 192 MiB of HBM per device.

```python
import math
import jax
import jax.numpy as jnp
import numpy as np
from jax import lax

D = 4096
HEADS = 32
KV_HEADS = 4
HD = 128
H_WIN = 768
TOPK = 8
TOK_DEV = 128
EXPERTS = 128
SLOT = 9
TOKENS = 16384
N_WIDE = 16
N_NARROW = 8


def shared_keys(key):
    return jnp.clip(jax.random.normal(key, (TOKENS, KV_HEADS, HD), jnp.float32), -6.0, 6.0)


def draw_keys(key, part):
    base = shared_keys(key)
    return base.astype(jnp.bfloat16)


def draw_queries(key, part):
    key = jax.random.fold_in(key, 5)
    base = jnp.clip(1.5 * jax.random.normal(key, (TOKENS, HEADS, HD), jnp.float32), -9.0, 9.0)
    return base.astype(jnp.bfloat16)


def level_of(key, shape, shards, low, top_value):
    def one(dim, parts):
        draws = jax.random.uniform(jax.random.fold_in(jax.random.fold_in(key, 6), dim), (parts,), jnp.float32, low / len(shards), top_value / len(shards))
        return jnp.repeat(jnp.exp(draws), shape[dim] // parts).reshape((-1,) + (1,) * (len(shape) - dim - 1))

    factor_of = one(*shards[0])
    for cut in shards[1:]:
        factor_of = factor_of * one(*cut)
    return factor_of


def shared_out(own_key, own, number, rows, number_of, top, most, slope):
    ranking = jax.random.permutation(own_key, number_of)
    heavy_load, common = portions_of(number_of, rows * top, most, slope, True), portions_of(number_of, rows * top, most, slope, False)
    places = jnp.arange(number_of)

    def named(tallies, offset_by):
        used = int((tallies > 0).sum())
        fixed = max(1, used // 4)
        shifted = fixed + (places - fixed + offset_by * (used - fixed)) % max(1, number_of - fixed)
        return jnp.zeros((number_of,), jnp.int32).at[ranking[jnp.where(places < fixed, places, shifted)]].set(jnp.asarray(tallies, jnp.int32))

    tallies = jnp.where(number % 4 == 0, named(heavy_load, number // 4), named(common, number - number // 4 - 1))
    mixed = jax.random.permutation(jax.random.fold_in(own, 3), number_of)
    source_of, receiver = mixed[0:number_of // 2 * 2:2], mixed[1:number_of // 2 * 2:2]
    margin = jnp.minimum(tallies[source_of] - 1, most - tallies[receiver]) // 2
    margin = jnp.where((source_of == ranking[0]) | (receiver == ranking[0]) | (tallies[receiver] == 0), 0, jnp.maximum(margin, 0))
    shifted = jax.random.randint(jax.random.fold_in(own, 4), (number_of // 2,), 0, 1 << 20) % (margin + 1)
    tallies = tallies.at[source_of].add(-shifted).at[receiver].add(shifted)
    items = jnp.searchsorted(jnp.cumsum(tallies), jnp.arange(rows * top), side="right").astype(jnp.int32)
    table = items.reshape(top, rows).T
    table = table[jax.random.permutation(jax.random.fold_in(own, 1), rows)]
    offset_by = jax.random.randint(jax.random.fold_in(own, 2), (rows, 1), 0, top)
    return jnp.take_along_axis(table, (jnp.arange(top)[None, :] + offset_by) % top, axis=1)


def portions_of(count, total, bound, lean, full):
    weights = [(1 << 20) // math.isqrt(standing ** lean) + 1 for standing in range(1, count + 1)]
    largest = bound if full else min(bound, max(-(-total // count), total * weights[0] // sum(weights)))
    least = 1 if total - largest >= count - 1 else 0
    given, rest = [largest] + [least] * (count - 1), total - largest - least * (count - 1)
    while rest > 0:
        candidates = [i for i in range(1, count) if given[i] < largest] or [i for i in range(1, count) if given[i] < bound]
        mass, remaining = sum([weights[i] for i in candidates]), rest
        for i in candidates:
            more = min(bound - given[i], max(1, remaining * weights[i] // mass), rest)
            given[i] = given[i] + more
            rest = rest - more
    return np.array(given)


def scatter_about(stream_key, dims, deviation, bound, shards=(), kind=jnp.bfloat16):
    factor_of = level_of(stream_key, dims, shards, -0.22, 0.18) if shards else 1.0
    array = jax.random.normal(stream_key, dims, jnp.float32) * deviation * factor_of
    return jnp.minimum(jnp.maximum(array, -bound), bound).astype(kind)


def setup_inputs(seed: int = 0) -> dict:
    key_of = jax.random.split(jax.random.key(seed), 12)
    queries = draw_queries(jax.random.fold_in(key_of[11], 71), 0)
    keys = draw_keys(jax.random.fold_in(key_of[11], 71), 0)
    values = scatter_about(key_of[2], (TOKENS, KV_HEADS, HD), 1.0, 6.0, ((0, 128),))
    residual = scatter_about(key_of[3], (TOKENS, D), 1.0, 6.0, ((0, 128),))
    out_proj = scatter_about(key_of[4], (HEADS * HD, D), (HEADS * HD) ** -0.5, 0.09375, ((0, 8),))
    norm_gain = jnp.clip(1.0 + 0.15 * jax.random.normal(key_of[5], (D,), jnp.float32), 0.25, 1.75)
    expert_ids_keys = jax.random.split(jax.random.fold_in(key_of[6], 1), TOKENS // TOK_DEV)
    expert_ids_turns = jax.random.permutation(jax.random.fold_in(key_of[6], 3), TOKENS // TOK_DEV)
    expert_ids = jax.vmap(lambda own, number: shared_out(jax.random.fold_in(key_of[6], 2), own, number, TOK_DEV, EXPERTS, TOPK, SLOT, 1))(expert_ids_keys, expert_ids_turns).reshape((TOKENS, TOPK))
    gate_weights = jnp.clip(jnp.exp(math.log(0.3) - 2.3025852 * jax.random.uniform(key_of[7], (TOKENS, TOPK), jnp.float32) ** level_of(key_of[7], (TOKENS, TOPK), ((0, 128),), -0.2, 0.2)), 0.03, 0.3)
    w_gate = scatter_about(key_of[8], (EXPERTS, D, H_WIN), D ** -0.5, 0.09375, ((0, 128),))
    w_up = scatter_about(key_of[9], (EXPERTS, D, H_WIN), D ** -0.5, 0.09375, ((0, 128),))
    w_down = scatter_about(key_of[10], (EXPERTS, H_WIN, D), H_WIN ** -0.5, 0.21875, ((0, 128),))
    return dict(queries=queries, keys=keys, values=values, residual=residual, out_proj=out_proj, norm_gain=norm_gain, expert_ids=expert_ids, gate_weights=gate_weights, w_gate=w_gate, w_up=w_up, w_down=w_down)


def attend(query_block, key_block, value_block):
    length = query_block.shape[0]
    kv_local = key_block.shape[1]
    per_kv = query_block.shape[1] // kv_local
    grouped = query_block.reshape(length, kv_local, per_kv, HD).astype(jnp.float32)
    scores = jnp.einsum('qkgd,skd->kgqs', grouped, key_block.astype(jnp.float32)) * (1.0 / math.sqrt(HD))
    causal = lax.broadcasted_iota(jnp.int32, (length, length), 0) >= lax.broadcasted_iota(jnp.int32, (length, length), 1)
    scores = jnp.where(causal, scores, -1e+30)
    highest = lax.optimization_barrier(jnp.max(scores, axis=-1, keepdims=True))
    weights = jnp.exp(scores - highest)
    probs = (weights / lax.optimization_barrier(jnp.sum(weights, axis=-1, keepdims=True))).astype(jnp.bfloat16)
    mixed = jnp.einsum('kgqs,skd->qkgd', probs.astype(jnp.float32), value_block.astype(jnp.float32))
    return mixed.astype(jnp.bfloat16).reshape(length, kv_local * per_kv * HD)

def reference(queries, keys, values, residual, out_proj, norm_gain, expert_ids, gate_weights, w_gate, w_up, w_down):
    length = N_NARROW * TOK_DEV
    group_cols = HEADS * HD // N_NARROW

    def one_sequence(seq_index):

        def take_rows(source):
            return lax.dynamic_slice_in_dim(source, seq_index * length, length, 0)
        attended = attend(take_rows(queries), take_rows(keys), take_rows(values))
        total = take_rows(residual).astype(jnp.float32)
        for group_index in range(N_NARROW):
            lo_col = group_index * group_cols
            partial_term = jnp.dot(attended[:, lo_col:lo_col + group_cols], out_proj[lo_col:lo_col + group_cols], preferred_element_type=jnp.float32)
            rounded = lax.optimization_barrier(partial_term.astype(jnp.bfloat16))
            total = total + rounded.astype(jnp.float32)
        return total
    hidden = lax.map(one_sequence, jnp.arange(N_WIDE, dtype=jnp.int32)).reshape(TOKENS, D)
    normed = (hidden * lax.rsqrt(lax.optimization_barrier(jnp.mean(hidden * hidden, axis=-1, keepdims=True)) + 1e-06) * norm_gain).astype(jnp.bfloat16)
    device_count = N_WIDE * N_NARROW
    buffer_rows = device_count * SLOT
    flat_ids = expert_ids.reshape(device_count, TOK_DEV * TOPK)
    one_hot = (flat_ids[:, :, None] == jnp.arange(EXPERTS, dtype=jnp.int32)[None, None, :]).astype(jnp.int32)
    rank = lax.optimization_barrier(jnp.sum(jnp.cumsum(one_hot, axis=1) * one_hot, axis=2)) - 1
    device_of = jnp.arange(device_count, dtype=jnp.int32)[:, None]
    slot = (flat_ids * buffer_rows + device_of * SLOT + rank).astype(jnp.int32).reshape(TOKENS, TOPK)
    source_token = jnp.broadcast_to(jnp.arange(TOKENS, dtype=jnp.int32)[:, None], (TOKENS, TOPK))
    table = jnp.full((EXPERTS * buffer_rows,), TOKENS, dtype=jnp.int32).at[slot.reshape(-1)].set(source_token.reshape(-1))
    padded = jnp.concatenate([normed, jnp.zeros((1, D), jnp.bfloat16)], axis=0)

    def one_expert(expert_index):
        rows_index = lax.dynamic_slice_in_dim(table, expert_index * buffer_rows, buffer_rows, 0)
        buffer = padded[rows_index]
        gated = jnp.dot(buffer, w_gate[expert_index], preferred_element_type=jnp.float32)
        upward = jnp.dot(buffer, w_up[expert_index], preferred_element_type=jnp.float32)
        inner = (jax.nn.silu(gated) * upward).astype(jnp.bfloat16)
        return jnp.dot(inner, w_down[expert_index], preferred_element_type=jnp.float32).astype(jnp.bfloat16)
    expert_out = lax.map(one_expert, jnp.arange(EXPERTS, dtype=jnp.int32)).reshape(EXPERTS * buffer_rows, D)
    mixture = jnp.zeros((TOKENS, D), jnp.float32)
    for choice_index in range(TOPK):
        mixture = mixture + gate_weights[:, choice_index:choice_index + 1] * expert_out[slot[:, choice_index]].astype(jnp.float32)
    return (hidden + mixture).astype(jnp.bfloat16)
```

```python
import math

import jax
import jax.numpy as jnp
import numpy as np
from jax import lax
from jax.experimental import pallas as pl
from jax.experimental.pallas import tpu as pltpu
from jax.sharding import PartitionSpec as P

MESH = pl.DeviceIdType.MESH
BF = jnp.bfloat16
F32 = jnp.float32


def offset_of(k):
    return k % 4, (k // 4 + k) % 4, (k // 16 + k // 4 + k) % 4, k // 64


def peer_of(k, sign):
    wide, narrow = lax.axis_index("wide"), lax.axis_index("narrow")
    dx, dy, dz, dc = offset_of(k)
    x = (wide // 4 + sign * dx + 4) % 4
    y = (wide % 4 + sign * dy + 4) % 4
    z = (narrow // 2 + sign * dz + 4) % 4
    c = (narrow % 2 + dc) % 2
    return (x * 4 + y, z * 2 + c)


def iota2(shape, dim):
    return lax.broadcasted_iota(jnp.int32, shape, dim)


def moe_kernel(
    normed,
    hidden,
    pick,
    pick8,
    mix_hi,
    mix_lo,
    mix8_hi,
    mix8_lo,
    wg_hbm,
    wu_hbm,
    wd_hbm,
    out,
    stage,
    recv,
    ret,
    wg,
    wu,
    wd,
    n2,
    g8,
    rows,
    inner,
    acc,
    w_sem,
    d_send,
    d_recv,
    r_send,
    r_recv,
):
    barrier = pltpu.get_barrier_semaphore()

    @pl.loop(1, 128)
    def _(k):
        pl.semaphore_signal(barrier, inc=1, device_id=peer_of(k, 1), device_id_type=MESH)

    loads = [
        pltpu.make_async_copy(src.at[0], dst, w_sem.at[i])
        for i, (src, dst) in enumerate(((wg_hbm, wg), (wu_hbm, wu), (wd_hbm, wd)))
    ]
    for load in loads:
        load.start()

    to_row = iota2((256, 256), 0)
    to_col = iota2((256, 256), 1)

    def folded(i):
        return ((i >> 3) & 15) * 16 + (i >> 7) * 8 + (i & 7)

    unfold = (to_col == folded(to_row)).astype(F32).astype(BF)
    fold = (to_row == folded(to_col)).astype(F32).astype(BF)
    swap = (to_col == (to_row & 15) * 16 + (to_row >> 4)).astype(F32).astype(BF)

    def dot(a, b):
        return jnp.dot(a, b, preferred_element_type=F32)

    def slab(k):
        return pl.ds(pl.multiple_of(k * 16, 16), 16)

    def group(q):
        return pl.ds(pl.multiple_of(q * 256, 256), 256)

    def dispatch(k):
        return pltpu.make_async_remote_copy(
            src_ref=stage.at[slab(k)],
            dst_ref=recv.at[slab(k)],
            send_sem=d_send.at[k],
            recv_sem=d_recv.at[k],
            device_id=peer_of(k, 1),
            device_id_type=MESH,
        )

    def give_back(k):
        return pltpu.make_async_remote_copy(
            src_ref=recv.at[slab(k)],
            dst_ref=ret.at[slab(k)],
            send_sem=r_send.at[k],
            recv_sem=r_recv.at[k],
            device_id=peer_of(k, -1),
            device_id_type=MESH,
        )

    own_in = pltpu.make_async_copy(stage.at[pl.ds(0, 16)], recv.at[pl.ds(0, 16)], d_recv.at[0])
    own_out = pltpu.make_async_copy(recv.at[pl.ds(0, 16)], ret.at[pl.ds(0, 16)], r_recv.at[0])

    n2[0:128, :] = normed[:, 0:2048]
    n2[128:256, :] = normed[:, 2048:4096]

    @pl.loop(0, 4)
    def _(n):
        cols = pl.ds(pl.multiple_of(n * 1024, 1024), 1024)
        g8[:, cols] = dot(pick8[...], normed[:, cols]).astype(BF)

    pl.semaphore_wait(barrier, 127)

    @pl.loop(0, 8)
    def _(q):
        for n in range(4):
            stage[group(q), n * 512 : (n + 1) * 512] = dot(
                pick[group(q), :], n2[:, n * 512 : (n + 1) * 512]
            ).astype(BF)
        some = g8[slab(q), :]
        piled = jnp.concatenate([some[:, g * 256 : (g + 1) * 256] for g in range(16)], axis=0)
        stage[group(q), 2048:2304] = dot(swap, piled).astype(BF)

        @pl.loop(0, 16)
        def _(i):
            k = q * 16 + i

            @pl.when(k > 0)
            def _():
                dispatch(k).start()

    own_in.start()
    for load in loads:
        load.wait()

    @pl.loop(0, 4)
    def _(j):
        @pl.loop(0, 32)
        def _(i):
            k = j * 32 + i

            @pl.when(k > 0)
            def _():
                dispatch(k).wait_recv()

            @pl.when(k == 0)
            def _():
                own_in.wait()

        for q in range(2):
            part = group(j * 2 + q)
            for n in range(4):
                cols = slice(n * 512, (n + 1) * 512)
                wide_rows = dot(unfold, recv[part, cols]).astype(BF)
                rows[q * 128 : (q + 1) * 128, n * 512 : (n + 1) * 512] = wide_rows[0:128]
                rows[q * 128 : (q + 1) * 128, 2048 + n * 512 : 2048 + (n + 1) * 512] = wide_rows[
                    128:256
                ]
            last = dot(swap, recv[part, 2048:2304]).astype(BF)
            for g in range(16):
                rows[256 + q * 16 : 272 + q * 16, g * 256 : (g + 1) * 256] = last[
                    g * 16 : (g + 1) * 16
                ]

        @pl.loop(0, 3)
        def _(n):
            cols = pl.ds(pl.multiple_of(n * 256, 256), 256)
            gated = dot(rows[...], wg[:, cols])
            upward = dot(rows[...], wu[:, cols])
            inner[:, cols] = (gated / (1.0 + jnp.exp(-gated)) * upward).astype(BF)

        @pl.loop(0, 8)
        def _(n):
            cols = pl.ds(pl.multiple_of(n * 512, 512), 512)
            rows[:, cols] = dot(inner[...], wd[:, cols]).astype(BF)

        for q in range(2):
            part = group(j * 2 + q)
            for n in range(4):
                piled = jnp.concatenate(
                    [
                        rows[q * 128 : (q + 1) * 128, n * 512 : (n + 1) * 512],
                        rows[q * 128 : (q + 1) * 128, 2048 + n * 512 : 2048 + (n + 1) * 512],
                    ],
                    axis=0,
                )
                recv[part, n * 512 : (n + 1) * 512] = dot(fold, piled).astype(BF)
            piled = jnp.concatenate(
                [
                    rows[256 + q * 16 : 272 + q * 16, g * 256 : (g + 1) * 256]
                    for g in range(16)
                ],
                axis=0,
            )
            recv[part, 2048:2304] = dot(swap, piled).astype(BF)

        @pl.loop(0, 32)
        def _(i):
            k = j * 32 + i

            @pl.when(k > 0)
            def _():
                give_back(k).start()

            @pl.when(k == 0)
            def _():
                own_out.start()

    acc[...] = jnp.zeros_like(acc)

    @pl.loop(0, 8)
    def _(q):
        @pl.loop(0, 16)
        def _(i):
            k = q * 16 + i

            @pl.when(k > 0)
            def _():
                give_back(k).wait_recv()

            @pl.when(k == 0)
            def _():
                own_out.wait()

        span = pl.ds(pl.multiple_of(q * 256, 256), 256)
        for n in range(4):
            cols = slice(n * 512, (n + 1) * 512)
            block = ret[group(q), cols]
            acc[:, cols] += dot(mix_hi[:, span], block) + dot(mix_lo[:, span], block)
        last = dot(swap, ret[group(q), 2048:2304]).astype(BF)
        for g in range(16):
            g8[slab(q), g * 256 : (g + 1) * 256] = last[g * 16 : (g + 1) * 16]

    for n in range(8):
        cols = slice(n * 512, (n + 1) * 512)
        half, inside = n // 4, slice((n % 4) * 512, (n % 4 + 1) * 512)
        block = g8[:, cols]
        total = acc[half * 128 : (half + 1) * 128, inside]
        total = total + dot(mix8_hi[...], block) + dot(mix8_lo[...], block)
        out[:, cols] = (hidden[:, cols] + total).astype(BF)

    @pl.loop(1, 128)
    def _(k):
        dispatch(k).wait_send()
        give_back(k).wait_send()


def moe(normed, hidden, expert_ids, gate_weights, w_gate, w_up, w_down):
    steps = jnp.arange(128, dtype=jnp.int32)
    wide, narrow = peer_of(steps, 1)
    expert_at = wide * 8 + narrow
    named = expert_ids[:, :, None] == expert_at[None, None, :]
    chosen = jnp.any(named, axis=1)
    weight = jnp.sum(jnp.where(named, gate_weights[:, :, None], 0.0), axis=1)
    before = iota2((128, 128), 0) > iota2((128, 128), 1)
    rank = jnp.dot(before.astype(BF), chosen.astype(BF), preferred_element_type=F32)
    rank = jnp.where(chosen, rank.astype(jnp.int32), -1)
    slots = jnp.arange(8, dtype=jnp.int32)
    at_slot = rank[:, :, None] == slots[None, None, :]
    mix = jnp.where(at_slot, weight[:, :, None], 0.0)

    def both_halves(a):
        zero = jnp.zeros_like(a)
        top = jnp.stack([a, zero], axis=2).reshape(128, 2048)
        low = jnp.stack([zero, a], axis=2).reshape(128, 2048)
        return jnp.concatenate([top, low], axis=0)

    pick = both_halves(at_slot.astype(BF)).T
    mix_hi = both_halves(mix).astype(BF)
    mix_lo = both_halves(mix - mix.astype(BF).astype(F32)).astype(BF)
    at_last = rank == 8
    pick8 = at_last.astype(BF).T
    mix8 = jnp.where(at_last, weight, 0.0)
    mix8_hi = mix8.astype(BF)
    mix8_lo = (mix8 - mix8_hi.astype(F32)).astype(BF)

    vmem = pl.BlockSpec(memory_space=pltpu.VMEM)
    hbm = pl.BlockSpec(memory_space=pl.ANY)
    return pl.pallas_call(
        moe_kernel,
        out_shape=jax.ShapeDtypeStruct((128, 4096), BF),
        in_specs=[vmem] * 8 + [hbm] * 3,
        out_specs=vmem,
        scratch_shapes=[
            pltpu.VMEM((2048, 2304), BF),
            pltpu.VMEM((2048, 2304), BF),
            pltpu.VMEM((2048, 2304), BF),
            pltpu.VMEM((4096, 768), BF),
            pltpu.VMEM((4096, 768), BF),
            pltpu.VMEM((768, 4096), BF),
            pltpu.VMEM((256, 2048), BF),
            pltpu.VMEM((128, 4096), BF),
            pltpu.VMEM((288, 4096), BF),
            pltpu.VMEM((288, 768), BF),
            pltpu.VMEM((256, 2048), F32),
            pltpu.SemaphoreType.DMA((3,)),
            pltpu.SemaphoreType.DMA((128,)),
            pltpu.SemaphoreType.DMA((128,)),
            pltpu.SemaphoreType.DMA((128,)),
            pltpu.SemaphoreType.DMA((128,)),
        ],
        compiler_params=pltpu.CompilerParams(
            collective_id=1, has_side_effects=True, vmem_limit_bytes=63 * 2**20
        ),
        cost_estimate=pl.CostEstimate(
            flops=25_000_000_000, bytes_accessed=25_000_000, transcendentals=1_000_000
        ),
    )(normed, hidden, pick, pick8, mix_hi, mix_lo, mix8_hi, mix8_lo, w_gate, w_up, w_down)


def attend(query_block, key_block, value_block):
    length = query_block.shape[0]
    kv_local = key_block.shape[1]
    per_kv = query_block.shape[1] // kv_local
    head_dim = query_block.shape[2]
    grouped = query_block.reshape(length, kv_local, per_kv, head_dim)
    scores = jnp.einsum(
        "qkgd,skd->kgqs", grouped, key_block, preferred_element_type=jnp.float32
    ) * (1.0 / math.sqrt(head_dim))
    causal = lax.broadcasted_iota(jnp.int32, (length, length), 0) >= lax.broadcasted_iota(
        jnp.int32, (length, length), 1
    )
    scores = jnp.where(causal, scores, -1e30)
    highest = jnp.max(scores, axis=-1, keepdims=True)
    weights = jnp.exp(scores - highest)
    probs = (weights / jnp.sum(weights, axis=-1, keepdims=True)).astype(jnp.bfloat16)
    mixed = jnp.einsum("kgqs,skd->qkgd", probs, value_block, preferred_element_type=jnp.float32)
    return mixed.astype(jnp.bfloat16).reshape(length, kv_local * per_kv * head_dim)


def shards(
    queries,
    keys,
    values,
    residual,
    out_proj,
    norm_gain,
    expert_ids,
    gate_weights,
    w_gate,
    w_up,
    w_down,
):
    narrow_count = lax.axis_size("narrow")
    head_count = queries.shape[1]
    kv_count = keys.shape[1]
    per_device = head_count // narrow_count
    group_size = head_count // kv_count
    kv_local = max(1, per_device // group_size)
    chosen_heads = np.concatenate(
        [
            np.arange(kv_local) + target_dev * per_device // group_size
            for target_dev in range(narrow_count)
        ]
    )
    query_group, key_group, value_group = (
        lax.all_to_all(queries, "narrow", split_axis=1, concat_axis=0, tiled=True),
        lax.all_to_all(keys[:, chosen_heads], "narrow", split_axis=1, concat_axis=0, tiled=True),
        lax.all_to_all(values[:, chosen_heads], "narrow", split_axis=1, concat_axis=0, tiled=True),
    )
    attended = attend(query_group, key_group, value_group)
    projected = lax.psum_scatter(
        jnp.dot(attended, out_proj, preferred_element_type=jnp.float32).astype(jnp.bfloat16),
        "narrow",
        scatter_dimension=0,
        tiled=True,
    ).astype(jnp.float32)
    hidden = residual.astype(jnp.float32) + projected
    normed = (
        hidden * lax.rsqrt(jnp.mean(hidden * hidden, axis=-1, keepdims=True) + 1e-06) * norm_gain
    ).astype(jnp.bfloat16)
    return moe(normed, hidden, expert_ids, gate_weights, w_gate, w_up, w_down)


def solution(mesh):
    in_specs = (
        P(("wide", "narrow"), None, None),
        P(("wide", "narrow"), None, None),
        P(("wide", "narrow"), None, None),
        P(("wide", "narrow"), None),
        P("narrow", None),
        P(),
        P(("wide", "narrow"), None),
        P(("wide", "narrow"), None),
        P(("wide", "narrow"), None, None),
        P(("wide", "narrow"), None, None),
        P(("wide", "narrow"), None, None),
    )
    out_specs = P(("wide", "narrow"), None)
    return jax.shard_map(shards, mesh=mesh, in_specs=in_specs, out_specs=out_specs, check_vma=False)
```

```python
import math

import jax
import jax.numpy as jnp
from jax import lax
from jax.experimental import pallas as pl
from jax.experimental.pallas import tpu as pltpu
from jax.sharding import PartitionSpec as P

MESH = pl.DeviceIdType.MESH
BF = jnp.bfloat16
F32 = jnp.float32


def offset_of(k):
    return k % 4, (k // 4 + k) % 4, (k // 16 + k // 4 + k) % 4, k // 64


def peer_of(k, sign):
    wide, narrow = lax.axis_index("wide"), lax.axis_index("narrow")
    dx, dy, dz, dc = offset_of(k)
    x = (wide // 4 + sign * dx + 4) % 4
    y = (wide % 4 + sign * dy + 4) % 4
    z = (narrow // 2 + sign * dz + 4) % 4
    c = (narrow % 2 + dc) % 2
    return (x * 4 + y, z * 2 + c)


def iota2(shape, dim):
    return lax.broadcasted_iota(jnp.int32, shape, dim)


def dot(a, b):
    return jnp.dot(a, b, preferred_element_type=F32)


def moe_kernel(
    normed,
    hidden,
    rank,
    rank_t,
    share_hi,
    share_lo,
    wg_hbm,
    wu_hbm,
    wd_hbm,
    out,
    stage,
    recv,
    ret,
    wg,
    wu,
    wd,
    n2,
    g8,
    rows,
    inner,
    acc,
    w_sem,
    d_send,
    d_recv,
    r_send,
    r_recv,
):
    barrier = pltpu.get_barrier_semaphore()

    @pl.loop(1, 128)
    def _(k):
        pl.semaphore_signal(barrier, inc=1, device_id=peer_of(k, 1), device_id_type=MESH)

    loads = [
        pltpu.make_async_copy(src.at[0], dst, w_sem.at[i])
        for i, (src, dst) in enumerate(((wg_hbm, wg), (wu_hbm, wu), (wd_hbm, wd)))
    ]
    for load in loads:
        load.start()

    to_row = iota2((256, 256), 0)
    to_col = iota2((256, 256), 1)

    def folded(i):
        return ((i >> 3) & 15) * 16 + (i >> 7) * 8 + (i & 7)

    def ones_where(mask):
        return jnp.where(mask, 1.0, 0.0).astype(BF)

    unfold = ones_where(to_col == folded(to_row))
    fold = ones_where(to_row == folded(to_col))
    swap = ones_where(to_col == (to_row & 15) * 16 + (to_row >> 4))

    def slab(k):
        return pl.ds(pl.multiple_of(k * 16, 16), 16)

    def group(q):
        return pl.ds(pl.multiple_of(q * 256, 256), 256)

    def dispatch(k):
        return pltpu.make_async_remote_copy(
            src_ref=stage.at[slab(k)],
            dst_ref=recv.at[slab(k)],
            send_sem=d_send.at[k],
            recv_sem=d_recv.at[k],
            device_id=peer_of(k, 1),
            device_id_type=MESH,
        )

    def give_back(k):
        return pltpu.make_async_remote_copy(
            src_ref=recv.at[slab(k)],
            dst_ref=ret.at[slab(k)],
            send_sem=r_send.at[k],
            recv_sem=r_recv.at[k],
            device_id=peer_of(k, -1),
            device_id_type=MESH,
        )

    own_in = pltpu.make_async_copy(stage.at[pl.ds(0, 16)], recv.at[pl.ds(0, 16)], d_recv.at[0])
    own_out = pltpu.make_async_copy(recv.at[pl.ds(0, 16)], ret.at[pl.ds(0, 16)], r_recv.at[0])

    n2[0:128, :] = normed[:, 0:2048]
    n2[128:256, :] = normed[:, 2048:4096]
    pick8 = ones_where(rank_t[...] == 8.0)

    @pl.loop(0, 4)
    def _(n):
        cols = pl.ds(pl.multiple_of(n * 1024, 1024), 1024)
        g8[:, cols] = dot(pick8, normed[:, cols]).astype(BF)

    spread_row, spread_col = iota2((256, 128), 0), iota2((256, 128), 1)
    slot_row = (spread_row & 7).astype(F32)
    low_row = (spread_row & 8) == 0

    pl.semaphore_wait(barrier, 127)

    @pl.loop(0, 8)
    def _(q):
        spread = ones_where((spread_row >> 4) + q * 16 == spread_col)
        hit = dot(spread, rank_t[...].astype(BF)) == slot_row
        pick = jnp.concatenate(
            [ones_where(hit & low_row), ones_where(hit & jnp.logical_not(low_row))], axis=1
        )
        for n in range(4):
            stage[group(q), n * 512 : (n + 1) * 512] = dot(
                pick, n2[:, n * 512 : (n + 1) * 512]
            ).astype(BF)
        some = g8[slab(q), :]
        piled = jnp.concatenate([some[:, g * 256 : (g + 1) * 256] for g in range(16)], axis=0)
        stage[group(q), 2048:2304] = dot(swap, piled).astype(BF)

        @pl.loop(0, 16)
        def _(i):
            k = q * 16 + i

            @pl.when(k > 0)
            def _():
                dispatch(k).start()

    own_in.start()
    for load in loads:
        load.wait()

    @pl.loop(0, 4)
    def _(j):
        @pl.loop(0, 32)
        def _(i):
            k = j * 32 + i

            @pl.when(k > 0)
            def _():
                dispatch(k).wait_recv()

            @pl.when(k == 0)
            def _():
                own_in.wait()

        for q in range(2):
            part = group(j * 2 + q)
            for n in range(4):
                cols = slice(n * 512, (n + 1) * 512)
                wide_rows = dot(unfold, recv[part, cols]).astype(BF)
                rows[q * 128 : (q + 1) * 128, n * 512 : (n + 1) * 512] = wide_rows[0:128]
                rows[q * 128 : (q + 1) * 128, 2048 + n * 512 : 2048 + (n + 1) * 512] = wide_rows[
                    128:256
                ]
            last = dot(swap, recv[part, 2048:2304]).astype(BF)
            for g in range(16):
                rows[256 + q * 16 : 272 + q * 16, g * 256 : (g + 1) * 256] = last[
                    g * 16 : (g + 1) * 16
                ]

        @pl.loop(0, 3)
        def _(n):
            cols = pl.ds(pl.multiple_of(n * 256, 256), 256)
            gated = dot(rows[...], wg[:, cols])
            upward = dot(rows[...], wu[:, cols])
            inner[:, cols] = (gated / (1.0 + jnp.exp(-gated)) * upward).astype(BF)

        @pl.loop(0, 8)
        def _(n):
            cols = pl.ds(pl.multiple_of(n * 512, 512), 512)
            rows[:, cols] = dot(inner[...], wd[:, cols]).astype(BF)

        for q in range(2):
            part = group(j * 2 + q)
            for n in range(4):
                piled = jnp.concatenate(
                    [
                        rows[q * 128 : (q + 1) * 128, n * 512 : (n + 1) * 512],
                        rows[q * 128 : (q + 1) * 128, 2048 + n * 512 : 2048 + (n + 1) * 512],
                    ],
                    axis=0,
                )
                recv[part, n * 512 : (n + 1) * 512] = dot(fold, piled).astype(BF)
            piled = jnp.concatenate(
                [
                    rows[256 + q * 16 : 272 + q * 16, g * 256 : (g + 1) * 256]
                    for g in range(16)
                ],
                axis=0,
            )
            recv[part, 2048:2304] = dot(swap, piled).astype(BF)

        @pl.loop(0, 32)
        def _(i):
            k = j * 32 + i

            @pl.when(k > 0)
            def _():
                give_back(k).start()

            @pl.when(k == 0)
            def _():
                own_out.start()

    acc[...] = jnp.zeros_like(acc)
    lane_row, lane_col = iota2((128, 256), 0), iota2((128, 256), 1)
    slot_col = (lane_col & 7).astype(F32)
    low_col = (lane_col & 8) == 0

    @pl.loop(0, 8)
    def _(q):
        @pl.loop(0, 16)
        def _(i):
            k = q * 16 + i

            @pl.when(k > 0)
            def _():
                give_back(k).wait_recv()

            @pl.when(k == 0)
            def _():
                own_out.wait()

        spread = ones_where((lane_col >> 4) + q * 16 == lane_row)
        hit = dot(rank[...].astype(BF), spread) == slot_col
        high = jnp.where(hit, dot(share_hi[...], spread), 0.0)
        low = jnp.where(hit, dot(share_lo[...], spread), 0.0)

        def both(a):
            return jnp.concatenate(
                [jnp.where(low_col, a, 0.0), jnp.where(low_col, 0.0, a)], axis=0
            ).astype(BF)

        mix_hi, mix_lo = both(high), both(low)
        for n in range(4):
            cols = slice(n * 512, (n + 1) * 512)
            block = ret[group(q), cols]
            acc[:, cols] += dot(mix_hi, block) + dot(mix_lo, block)
        last = dot(swap, ret[group(q), 2048:2304]).astype(BF)
        for g in range(16):
            g8[slab(q), g * 256 : (g + 1) * 256] = last[g * 16 : (g + 1) * 16]

    at_last = rank[...] == 8.0
    mix8_hi = jnp.where(at_last, share_hi[...].astype(F32), 0.0).astype(BF)
    mix8_lo = jnp.where(at_last, share_lo[...].astype(F32), 0.0).astype(BF)
    for n in range(8):
        cols = slice(n * 512, (n + 1) * 512)
        half, inside = n // 4, slice((n % 4) * 512, (n % 4 + 1) * 512)
        block = g8[:, cols]
        total = acc[half * 128 : (half + 1) * 128, inside]
        total = total + dot(mix8_hi, block) + dot(mix8_lo, block)
        out[:, cols] = (hidden[:, cols] + total).astype(BF)

    @pl.loop(1, 128)
    def _(k):
        dispatch(k).wait_send()
        give_back(k).wait_send()


def moe(normed, hidden, expert_ids, gate_weights, w_gate, w_up, w_down):
    steps = jnp.arange(128, dtype=jnp.int32)
    wide, narrow = peer_of(steps, 1)
    expert_at = wide * 8 + narrow
    named = expert_ids[:, :, None] == expert_at[None, None, :]
    chosen = jnp.any(named, axis=1)
    share = jnp.sum(jnp.where(named, gate_weights[:, :, None], 0.0), axis=1)
    before = iota2((128, 128), 0) > iota2((128, 128), 1)
    rank = jnp.where(chosen, dot(before.astype(BF), chosen.astype(BF)), -1.0)
    share_hi = share.astype(BF)
    share_lo = (share - share_hi.astype(F32)).astype(BF)

    vmem = pl.BlockSpec(memory_space=pltpu.VMEM)
    hbm = pl.BlockSpec(memory_space=pl.ANY)
    return pl.pallas_call(
        moe_kernel,
        out_shape=jax.ShapeDtypeStruct((128, 4096), BF),
        in_specs=[vmem] * 6 + [hbm] * 3,
        out_specs=vmem,
        scratch_shapes=[
            pltpu.VMEM((2048, 2304), BF),
            pltpu.VMEM((2048, 2304), BF),
            pltpu.VMEM((2048, 2304), BF),
            pltpu.VMEM((4096, 768), BF),
            pltpu.VMEM((4096, 768), BF),
            pltpu.VMEM((768, 4096), BF),
            pltpu.VMEM((256, 2048), BF),
            pltpu.VMEM((128, 4096), BF),
            pltpu.VMEM((288, 4096), BF),
            pltpu.VMEM((288, 768), BF),
            pltpu.VMEM((256, 2048), F32),
            pltpu.SemaphoreType.DMA((3,)),
            pltpu.SemaphoreType.DMA((128,)),
            pltpu.SemaphoreType.DMA((128,)),
            pltpu.SemaphoreType.DMA((128,)),
            pltpu.SemaphoreType.DMA((128,)),
        ],
        compiler_params=pltpu.CompilerParams(
            collective_id=1, has_side_effects=True, vmem_limit_bytes=62 * 2**20
        ),
        cost_estimate=pl.CostEstimate(
            flops=25_000_000_000, bytes_accessed=25_000_000, transcendentals=1_000_000
        ),
    )(normed, hidden, rank, rank.T, share_hi, share_lo, w_gate, w_up, w_down)


def front_kernel(
    q_in,
    kv_in,
    residual,
    proj_hbm,
    gain,
    hidden,
    normed,
    q_all,
    kv_all,
    proj,
    mixed,
    keep,
    give,
    sib,
    relay_out,
    relay_in,
    sums,
    land,
    w_sem,
    q_send,
    q_recv,
    kv_send,
    kv_recv,
    s_send,
    s_recv,
    y_send,
    y_recv,
    l_send,
    l_recv,
):
    wide, narrow = lax.axis_index("wide"), lax.axis_index("narrow")
    z, c = narrow // 2, narrow % 2

    def at(dz, dc):
        return ((z + dz) % 4) * 2 + (c + dc) % 2

    barrier = pltpu.get_barrier_semaphore()
    for s in range(1, 8):
        pl.semaphore_signal(
            barrier, inc=1, device_id=(wide, at(s // 2, s % 2)), device_id_type=MESH
        )
    load = pltpu.make_async_copy(proj_hbm, proj, w_sem.at[0])
    load.start()

    def mine(start):
        return pl.ds(pl.multiple_of(start * 128, 128), 128)

    def send_q(s):
        to = at(s // 2, s % 2)
        return pltpu.make_async_remote_copy(
            src_ref=q_in.at[to],
            dst_ref=q_all.at[narrow],
            send_sem=q_send.at[s],
            recv_sem=q_recv.at[s],
            device_id=(wide, to),
            device_id_type=MESH,
        )

    def send_kv(s):
        to = at(s // 2, s % 2)
        return pltpu.make_async_remote_copy(
            src_ref=kv_in.at[to // 2],
            dst_ref=kv_all.at[:, mine(narrow), :],
            send_sem=kv_send.at[s],
            recv_sem=kv_recv.at[s],
            device_id=(wide, to),
            device_id_type=MESH,
        )

    own_q = pltpu.make_async_copy(q_in.at[narrow], q_all.at[narrow], q_recv.at[0])
    own_kv = pltpu.make_async_copy(kv_in.at[z], kv_all.at[:, mine(narrow), :], kv_recv.at[0])
    own_q.start()
    own_kv.start()
    pl.semaphore_wait(barrier, 7)
    for s in (4, 5, 2, 6, 3, 7, 1):
        send_kv(s).start()
    for s in (4, 5, 2, 6, 3, 7, 1):
        send_q(s).start()

    def to_sibling(i):
        return pltpu.make_async_remote_copy(
            src_ref=give.at[i],
            dst_ref=sib.at[i],
            send_sem=s_send.at[i],
            recv_sem=s_recv.at[i],
            device_id=(wide, at(0, 1)),
            device_id_type=MESH,
        )

    def to_relay(i):
        return pltpu.make_async_remote_copy(
            src_ref=relay_out.at[i],
            dst_ref=relay_in.at[i],
            send_sem=y_send.at[i],
            recv_sem=y_recv.at[i],
            device_id=(wide, at((1, 3)[i], 0)),
            device_id_type=MESH,
        )

    def to_owner(i):
        return pltpu.make_async_remote_copy(
            src_ref=sums.at[i],
            dst_ref=land.at[i],
            send_sem=l_send.at[i],
            recv_sem=l_recv.at[i],
            device_id=(wide, at((1, 3)[i], 0)),
            device_id_type=MESH,
        )

    own_kv.wait()
    for s in range(1, 8):
        send_kv(s).wait_recv()
    load.wait()

    scale = math.log2(math.e) / math.sqrt(128)
    q_row, k_col = iota2((256, 1024), 0) & 127, iota2((256, 1024), 1)

    def partial(i):
        dz = (2, 1, 3, 0)[i]
        back = (4 - dz) % 4
        for s in (back * 2, back * 2 + 1):
            if s == 0:
                own_q.wait()
            else:
                send_q(s).wait_recv()

        @pl.loop(0, 4)
        def _(step):
            block = at(dz, step // 2)
            part = pl.ds(pl.multiple_of((step % 2) * 256, 256), 256)
            query = q_all[block, part, :]
            scores = lax.dot_general(
                query, kv_all[0], (((1,), (1,)), ((), ())), preferred_element_type=F32
            )
            scores = jnp.where(q_row + block * 128 >= k_col, scores, -1e30)
            highest = jnp.max(scores, axis=-1, keepdims=True)
            weights = jnp.exp2((scores - highest) * scale)
            total = jnp.sum(weights, axis=-1, keepdims=True)
            both = (dot(weights.astype(BF), kv_all[1]) / total).astype(BF)
            down = mine(step // 2)
            mixed[down, pl.ds(pl.multiple_of((step % 2) * 256, 256), 128)] = both[0:128]
            mixed[down, pl.ds(pl.multiple_of((step % 2) * 256 + 128, 128), 128)] = both[128:256]

        @pl.loop(0, 4)
        def _(n):
            cols = pl.ds(pl.multiple_of(n * 1024, 1024), 1024)
            term = dot(mixed[...], proj[:, cols]).astype(BF)
            keep[i, :, cols] = term[0:128]
            give[i, :, cols] = term[128:256]

        to_sibling(i).start()

    left, right = slice(0, 2048), slice(2048, 4096)

    def pair(i, cols):
        return keep[i, :, cols].astype(F32) + sib[i, :, cols].astype(F32)

    partial(0)
    partial(1)
    to_sibling(0).wait_recv()
    relay_out[0] = pair(0, left).astype(BF)
    to_relay(0).start()
    relay_out[1] = pair(0, right).astype(BF)
    to_relay(1).start()
    partial(2)
    to_sibling(1).wait_recv()
    sums[0, :, right] = pair(1, right).astype(BF)
    to_relay(0).wait_recv()
    sums[0, :, left] = (pair(1, left) + relay_in[0].astype(F32)).astype(BF)
    to_owner(0).start()
    to_sibling(2).wait_recv()
    sums[1, :, left] = pair(2, left).astype(BF)
    to_relay(1).wait_recv()
    sums[1, :, right] = (pair(2, right) + relay_in[1].astype(F32)).astype(BF)
    to_owner(1).start()
    partial(3)
    to_sibling(3).wait_recv()
    for n in range(4):
        cols = slice(n * 1024, (n + 1) * 1024)
        hidden[:, cols] = residual[:, cols].astype(F32) + pair(3, cols)
    to_owner(0).wait_recv()
    to_owner(1).wait_recv()
    square = jnp.zeros((128, 1), F32)
    for n in range(4):
        cols = slice(n * 1024, (n + 1) * 1024)
        full = hidden[:, cols] + (land[0, :, cols].astype(F32) + land[1, :, cols].astype(F32))
        hidden[:, cols] = full
        square = square + jnp.sum(full * full, axis=-1, keepdims=True)
    factor = lax.rsqrt(square * (1.0 / 4096) + 1e-06)
    for n in range(4):
        cols = slice(n * 1024, (n + 1) * 1024)
        normed[:, cols] = (hidden[:, cols] * factor * gain[:, cols]).astype(BF)

    for s in range(1, 8):
        send_kv(s).wait_send()
        send_q(s).wait_send()
    for i in range(4):
        to_sibling(i).wait_send()
    for i in range(2):
        to_relay(i).wait_send()
        to_owner(i).wait_send()


def front(queries, keys, values, residual, out_proj, norm_gain):
    q_in = jnp.transpose(queries, (1, 0, 2)).reshape(8, 512, 128)
    kv_in = jnp.transpose(jnp.stack([keys, values]), (2, 0, 1, 3))
    vmem = pl.BlockSpec(memory_space=pltpu.VMEM)
    hbm = pl.BlockSpec(memory_space=pl.ANY)
    return pl.pallas_call(
        front_kernel,
        out_shape=(
            jax.ShapeDtypeStruct((128, 4096), F32),
            jax.ShapeDtypeStruct((128, 4096), BF),
        ),
        in_specs=[hbm, hbm, vmem, hbm, vmem],
        out_specs=(vmem, vmem),
        scratch_shapes=[
            pltpu.VMEM((8, 512, 128), BF),
            pltpu.VMEM((2, 1024, 128), BF),
            pltpu.VMEM((512, 4096), BF),
            pltpu.VMEM((256, 512), BF),
            pltpu.VMEM((4, 128, 4096), BF),
            pltpu.VMEM((4, 128, 4096), BF),
            pltpu.VMEM((4, 128, 4096), BF),
            pltpu.VMEM((2, 128, 2048), BF),
            pltpu.VMEM((2, 128, 2048), BF),
            pltpu.VMEM((2, 128, 4096), BF),
            pltpu.VMEM((2, 128, 4096), BF),
            pltpu.SemaphoreType.DMA((1,)),
            pltpu.SemaphoreType.DMA((8,)),
            pltpu.SemaphoreType.DMA((8,)),
            pltpu.SemaphoreType.DMA((8,)),
            pltpu.SemaphoreType.DMA((8,)),
            pltpu.SemaphoreType.DMA((4,)),
            pltpu.SemaphoreType.DMA((4,)),
            pltpu.SemaphoreType.DMA((2,)),
            pltpu.SemaphoreType.DMA((2,)),
            pltpu.SemaphoreType.DMA((2,)),
            pltpu.SemaphoreType.DMA((2,)),
        ],
        compiler_params=pltpu.CompilerParams(
            collective_id=0, has_side_effects=True, vmem_limit_bytes=48 * 2**20
        ),
        cost_estimate=pl.CostEstimate(
            flops=7_000_000_000, bytes_accessed=9_000_000, transcendentals=4_000_000
        ),
    )(q_in, kv_in, residual, out_proj, norm_gain.reshape(1, 4096))


def shards(
    queries,
    keys,
    values,
    residual,
    out_proj,
    norm_gain,
    expert_ids,
    gate_weights,
    w_gate,
    w_up,
    w_down,
):
    hidden, normed = front(queries, keys, values, residual, out_proj, norm_gain)
    return moe(normed, hidden, expert_ids, gate_weights, w_gate, w_up, w_down)


def solution(mesh):
    in_specs = (
        P(("wide", "narrow"), None, None),
        P(("wide", "narrow"), None, None),
        P(("wide", "narrow"), None, None),
        P(("wide", "narrow"), None),
        P("narrow", None),
        P(),
        P(("wide", "narrow"), None),
        P(("wide", "narrow"), None),
        P(("wide", "narrow"), None, None),
        P(("wide", "narrow"), None, None),
        P(("wide", "narrow"), None, None),
    )
    out_specs = P(("wide", "narrow"), None)
    return jax.shard_map(shards, mesh=mesh, in_specs=in_specs, out_specs=out_specs, check_vma=False)
```

```python
import math

import jax
import jax.numpy as jnp
from jax import lax
from jax.experimental import pallas as pl
from jax.experimental.pallas import tpu as pltpu
from jax.sharding import PartitionSpec as P

MESH = pl.DeviceIdType.MESH
BF = jnp.bfloat16
F32 = jnp.float32


def offset_of(k):
    j = (128 - k) & 127
    return j, (j >> 2) + j, (j >> 4) + (j >> 2) + j, j >> 6


def peer_of(k, sign):
    wide, narrow = lax.axis_index("wide"), lax.axis_index("narrow")
    dx, dy, dz, dc = offset_of(k)
    x = ((wide >> 2) + sign * dx) & 3
    y = (wide + sign * dy) & 3
    z = ((narrow >> 1) + sign * dz) & 3
    c = (narrow + dc) & 1
    return (x * 4 + y, z * 2 + c)


def iota2(shape, dim):
    return lax.broadcasted_iota(jnp.int32, shape, dim)


def dot(a, b):
    return jnp.dot(a, b, preferred_element_type=F32)


def moe_kernel(
    normed,
    hidden,
    rank,
    rank_t,
    share_hi,
    share_lo,
    wg_hbm,
    wu_hbm,
    wd_hbm,
    out,
    stage,
    recv,
    ret,
    wg,
    wu,
    wd,
    n2,
    g8,
    rows,
    inner,
    acc,
    row_in,
    w_sem,
    d_send,
    d_recv,
    r_send,
    r_recv,
):
    wide, narrow = lax.axis_index("wide"), lax.axis_index("narrow")
    barrier = pltpu.get_barrier_semaphore()
    for d in range(1, 8):
        pl.semaphore_signal(
            barrier, inc=1, device_id=(wide, (narrow + d) & 7), device_id_type=MESH
        )
    for d in range(1, 16):
        pl.semaphore_signal(
            barrier, inc=1, device_id=((wide + d) & 15, narrow), device_id_type=MESH
        )

    loads = [
        pltpu.make_async_copy(src.at[0], dst, w_sem.at[i])
        for i, (src, dst) in enumerate(((wg_hbm, wg), (wu_hbm, wu), (wd_hbm, wd)))
    ]
    for load in loads:
        load.start()

    to_row = iota2((256, 256), 0)
    to_col = iota2((256, 256), 1)

    def folded(i):
        return ((i >> 3) & 15) * 16 + (i >> 7) * 8 + (i & 7)

    def ones_where(mask):
        return jnp.where(mask, 1.0, 0.0).astype(BF)

    unfold = ones_where(to_col == folded(to_row))
    fold = ones_where(to_row == folded(to_col))
    swap = ones_where(to_col == (to_row & 15) * 16 + (to_row >> 4))

    def slab(k):
        return pl.ds(pl.multiple_of(k * 16, 16), 16)

    def group(q):
        return pl.ds(pl.multiple_of(q * 256, 256), 256)

    def dispatch(k):
        return pltpu.make_async_remote_copy(
            src_ref=stage.at[slab(k)],
            dst_ref=recv.at[slab(k)],
            send_sem=d_send.at[k],
            recv_sem=d_recv.at[k],
            device_id=peer_of(k, 1),
            device_id_type=MESH,
        )

    def give_back(k):
        return pltpu.make_async_remote_copy(
            src_ref=recv.at[slab(k)],
            dst_ref=ret.at[slab(k)],
            send_sem=r_send.at[k],
            recv_sem=r_recv.at[k],
            device_id=peer_of(k, -1),
            device_id_type=MESH,
        )

    own_in = pltpu.make_async_copy(stage.at[pl.ds(0, 16)], recv.at[pl.ds(0, 16)], d_recv.at[0])
    own_out = pltpu.make_async_copy(recv.at[pl.ds(0, 16)], ret.at[pl.ds(0, 16)], r_recv.at[0])

    n2[0:128, :] = normed[:, 0:2048]
    n2[128:256, :] = normed[:, 2048:4096]
    pick8 = ones_where(rank_t[...] == 8.0)

    @pl.loop(0, 4)
    def _(n):
        cols = pl.ds(pl.multiple_of(n * 1024, 1024), 1024)
        g8[:, cols] = dot(pick8, normed[:, cols]).astype(BF)

    spread_row, spread_col = iota2((256, 128), 0), iota2((256, 128), 1)
    slot_row = (spread_row & 7).astype(F32)
    low_row = (spread_row & 8) == 0

    pl.semaphore_wait(barrier, 22)
    for d in range(1, 8):
        pl.semaphore_signal(row_in, inc=1, device_id=(wide, (narrow + d) & 7), device_id_type=MESH)
    pl.semaphore_wait(row_in, 7)

    @pl.loop(0, 8)
    def _(q):
        spread = ones_where((spread_row >> 4) + q * 16 == spread_col)
        hit = dot(spread, rank_t[...].astype(BF)) == slot_row
        pick = jnp.concatenate(
            [ones_where(hit & low_row), ones_where(hit & jnp.logical_not(low_row))], axis=1
        )
        for n in range(4):
            stage[group(q), n * 512 : (n + 1) * 512] = dot(
                pick, n2[:, n * 512 : (n + 1) * 512]
            ).astype(BF)
        some = g8[slab(q), :]
        piled = jnp.concatenate([some[:, g * 256 : (g + 1) * 256] for g in range(16)], axis=0)
        stage[group(q), 2048:2304] = dot(swap, piled).astype(BF)

        @pl.loop(0, 16)
        def _(i):
            k = q * 16 + i

            @pl.when(k > 0)
            def _():
                dispatch(k).start()

    own_in.start()
    for load in loads:
        load.wait()

    @pl.loop(0, 4)
    def _(j):
        @pl.loop(0, 32)
        def _(i):
            k = j * 32 + i

            @pl.when(k > 0)
            def _():
                dispatch(k).wait_recv()

            @pl.when(k == 0)
            def _():
                own_in.wait()

        for q in range(2):
            part = group(j * 2 + q)
            for n in range(4):
                cols = slice(n * 512, (n + 1) * 512)
                wide_rows = dot(unfold, recv[part, cols]).astype(BF)
                rows[q * 128 : (q + 1) * 128, n * 512 : (n + 1) * 512] = wide_rows[0:128]
                rows[q * 128 : (q + 1) * 128, 2048 + n * 512 : 2048 + (n + 1) * 512] = wide_rows[
                    128:256
                ]
            last = dot(swap, recv[part, 2048:2304]).astype(BF)
            for g in range(16):
                rows[256 + q * 16 : 272 + q * 16, g * 256 : (g + 1) * 256] = last[
                    g * 16 : (g + 1) * 16
                ]

        @pl.loop(0, 3)
        def _(n):
            cols = pl.ds(pl.multiple_of(n * 256, 256), 256)
            gated = dot(rows[...], wg[:, cols])
            upward = dot(rows[...], wu[:, cols])
            inner[:, cols] = (gated / (1.0 + jnp.exp(-gated)) * upward).astype(BF)

        @pl.loop(0, 8)
        def _(n):
            cols = pl.ds(pl.multiple_of(n * 512, 512), 512)
            rows[:, cols] = dot(inner[...], wd[:, cols]).astype(BF)

        for q in range(2):
            part = group(j * 2 + q)
            for n in range(4):
                piled = jnp.concatenate(
                    [
                        rows[q * 128 : (q + 1) * 128, n * 512 : (n + 1) * 512],
                        rows[q * 128 : (q + 1) * 128, 2048 + n * 512 : 2048 + (n + 1) * 512],
                    ],
                    axis=0,
                )
                recv[part, n * 512 : (n + 1) * 512] = dot(fold, piled).astype(BF)
            piled = jnp.concatenate(
                [
                    rows[256 + q * 16 : 272 + q * 16, g * 256 : (g + 1) * 256]
                    for g in range(16)
                ],
                axis=0,
            )
            recv[part, 2048:2304] = dot(swap, piled).astype(BF)

        @pl.loop(0, 32)
        def _(i):
            k = j * 32 + i

            @pl.when(k > 0)
            def _():
                give_back(k).start()

            @pl.when(k == 0)
            def _():
                own_out.start()

    acc[...] = jnp.zeros_like(acc)
    lane_row, lane_col = iota2((128, 256), 0), iota2((128, 256), 1)
    slot_col = (lane_col & 7).astype(F32)
    low_col = (lane_col & 8) == 0

    @pl.loop(0, 8)
    def _(q):
        @pl.loop(0, 16)
        def _(i):
            k = q * 16 + i

            @pl.when(k > 0)
            def _():
                give_back(k).wait_recv()

            @pl.when(k == 0)
            def _():
                own_out.wait()

        spread = ones_where((lane_col >> 4) + q * 16 == lane_row)
        hit = dot(rank[...].astype(BF), spread) == slot_col
        high = jnp.where(hit, dot(share_hi[...], spread), 0.0)
        low = jnp.where(hit, dot(share_lo[...], spread), 0.0)

        def both(a):
            return jnp.concatenate(
                [jnp.where(low_col, a, 0.0), jnp.where(low_col, 0.0, a)], axis=0
            ).astype(BF)

        mix_hi, mix_lo = both(high), both(low)
        for n in range(4):
            cols = slice(n * 512, (n + 1) * 512)
            block = ret[group(q), cols]
            acc[:, cols] += dot(mix_hi, block) + dot(mix_lo, block)
        last = dot(swap, ret[group(q), 2048:2304]).astype(BF)
        for g in range(16):
            g8[slab(q), g * 256 : (g + 1) * 256] = last[g * 16 : (g + 1) * 16]

    at_last = rank[...] == 8.0
    mix8_hi = jnp.where(at_last, share_hi[...].astype(F32), 0.0).astype(BF)
    mix8_lo = jnp.where(at_last, share_lo[...].astype(F32), 0.0).astype(BF)
    for n in range(8):
        cols = slice(n * 512, (n + 1) * 512)
        half, inside = n // 4, slice((n % 4) * 512, (n % 4 + 1) * 512)
        block = g8[:, cols]
        total = acc[half * 128 : (half + 1) * 128, inside]
        total = total + dot(mix8_hi, block) + dot(mix8_lo, block)
        out[:, cols] = (hidden[:, cols] + total).astype(BF)

    @pl.loop(1, 128)
    def _(k):
        dispatch(k).wait_send()
        give_back(k).wait_send()


def moe(normed, hidden, expert_ids, gate_weights, w_gate, w_up, w_down):
    steps = jnp.arange(128, dtype=jnp.int32)
    wide, narrow = peer_of(steps, 1)
    expert_at = wide * 8 + narrow
    named = expert_ids[:, :, None] == expert_at[None, None, :]
    chosen = jnp.any(named, axis=1)
    share = jnp.sum(jnp.where(named, gate_weights[:, :, None], 0.0), axis=1)
    before = iota2((128, 128), 0) > iota2((128, 128), 1)
    rank = jnp.where(chosen, dot(before.astype(BF), chosen.astype(BF)), -1.0)
    share_hi = share.astype(BF)
    share_lo = (share - share_hi.astype(F32)).astype(BF)

    vmem = pl.BlockSpec(memory_space=pltpu.VMEM)
    hbm = pl.BlockSpec(memory_space=pl.ANY)
    return pl.pallas_call(
        moe_kernel,
        out_shape=jax.ShapeDtypeStruct((128, 4096), BF),
        in_specs=[vmem] * 6 + [hbm] * 3,
        out_specs=vmem,
        scratch_shapes=[
            pltpu.VMEM((2048, 2304), BF),
            pltpu.VMEM((2048, 2304), BF),
            pltpu.VMEM((2048, 2304), BF),
            pltpu.VMEM((4096, 768), BF),
            pltpu.VMEM((4096, 768), BF),
            pltpu.VMEM((768, 4096), BF),
            pltpu.VMEM((256, 2048), BF),
            pltpu.VMEM((128, 4096), BF),
            pltpu.VMEM((288, 4096), BF),
            pltpu.VMEM((288, 768), BF),
            pltpu.VMEM((256, 2048), F32),
            pltpu.SemaphoreType.REGULAR,
            pltpu.SemaphoreType.DMA((3,)),
            pltpu.SemaphoreType.DMA((128,)),
            pltpu.SemaphoreType.DMA((128,)),
            pltpu.SemaphoreType.DMA((128,)),
            pltpu.SemaphoreType.DMA((128,)),
        ],
        compiler_params=pltpu.CompilerParams(
            collective_id=1, has_side_effects=True, vmem_limit_bytes=62 * 2**20
        ),
        cost_estimate=pl.CostEstimate(
            flops=25_000_000_000, bytes_accessed=25_000_000, transcendentals=1_000_000
        ),
    )(normed, hidden, rank, rank.T, share_hi, share_lo, w_gate, w_up, w_down)


def front_kernel(
    q_in,
    kv_in,
    residual,
    proj_hbm,
    gain,
    hidden,
    normed,
    q_all,
    kv_all,
    proj,
    mixed,
    keep,
    give,
    sib,
    relay_out,
    relay_in,
    sums,
    land,
    w_sem,
    q_send,
    q_recv,
    kv_send,
    kv_recv,
    s_send,
    s_recv,
    y_send,
    y_recv,
    l_send,
    l_recv,
):
    wide, narrow = lax.axis_index("wide"), lax.axis_index("narrow")
    z, c = narrow // 2, narrow % 2

    def at(dz, dc):
        return ((z + dz) % 4) * 2 + (c + dc) % 2

    barrier = pltpu.get_barrier_semaphore()
    for s in range(1, 8):
        pl.semaphore_signal(
            barrier, inc=1, device_id=(wide, at(s // 2, s % 2)), device_id_type=MESH
        )
    load = pltpu.make_async_copy(proj_hbm, proj, w_sem.at[0])
    load.start()

    def mine(start):
        return pl.ds(pl.multiple_of(start * 128, 128), 128)

    def send_q(s):
        to = at(s // 2, s % 2)
        return pltpu.make_async_remote_copy(
            src_ref=q_in.at[to],
            dst_ref=q_all.at[narrow],
            send_sem=q_send.at[s],
            recv_sem=q_recv.at[s],
            device_id=(wide, to),
            device_id_type=MESH,
        )

    def send_kv(s):
        to = at(s // 2, s % 2)
        return pltpu.make_async_remote_copy(
            src_ref=kv_in.at[to // 2],
            dst_ref=kv_all.at[:, mine(narrow), :],
            send_sem=kv_send.at[s],
            recv_sem=kv_recv.at[s],
            device_id=(wide, to),
            device_id_type=MESH,
        )

    own_q = pltpu.make_async_copy(q_in.at[narrow], q_all.at[narrow], q_recv.at[0])
    own_kv = pltpu.make_async_copy(kv_in.at[z], kv_all.at[:, mine(narrow), :], kv_recv.at[0])
    own_q.start()
    own_kv.start()
    pl.semaphore_wait(barrier, 7)
    for s in (4, 5, 2, 6, 3, 7, 1):
        send_kv(s).start()
    for s in (4, 5, 2, 6, 3, 7, 1):
        send_q(s).start()

    def to_sibling(i):
        return pltpu.make_async_remote_copy(
            src_ref=give.at[i],
            dst_ref=sib.at[i],
            send_sem=s_send.at[i],
            recv_sem=s_recv.at[i],
            device_id=(wide, at(0, 1)),
            device_id_type=MESH,
        )

    def to_relay(i):
        return pltpu.make_async_remote_copy(
            src_ref=relay_out.at[i],
            dst_ref=relay_in.at[i],
            send_sem=y_send.at[i],
            recv_sem=y_recv.at[i],
            device_id=(wide, at((1, 3)[i], 0)),
            device_id_type=MESH,
        )

    def to_owner(i):
        return pltpu.make_async_remote_copy(
            src_ref=sums.at[i],
            dst_ref=land.at[i],
            send_sem=l_send.at[i],
            recv_sem=l_recv.at[i],
            device_id=(wide, at((1, 3)[i], 0)),
            device_id_type=MESH,
        )

    own_kv.wait()
    for s in range(1, 8):
        send_kv(s).wait_recv()
    load.wait()

    scale = math.log2(math.e) / math.sqrt(128)
    q_row, k_col = iota2((256, 1024), 0) & 127, iota2((256, 1024), 1)

    def partial(i):
        dz = (2, 1, 3, 0)[i]
        back = (4 - dz) % 4
        for s in (back * 2, back * 2 + 1):
            if s == 0:
                own_q.wait()
            else:
                send_q(s).wait_recv()

        @pl.loop(0, 4)
        def _(step):
            block = at(dz, step // 2)
            part = pl.ds(pl.multiple_of((step % 2) * 256, 256), 256)
            query = q_all[block, part, :]
            scores = lax.dot_general(
                query, kv_all[0], (((1,), (1,)), ((), ())), preferred_element_type=F32
            )
            scores = jnp.where(q_row + block * 128 >= k_col, scores, -1e30)
            highest = jnp.max(scores, axis=-1, keepdims=True)
            weights = jnp.exp2((scores - highest) * scale)
            total = jnp.sum(weights, axis=-1, keepdims=True)
            both = (dot(weights.astype(BF), kv_all[1]) / total).astype(BF)
            down = mine(step // 2)
            mixed[down, pl.ds(pl.multiple_of((step % 2) * 256, 256), 128)] = both[0:128]
            mixed[down, pl.ds(pl.multiple_of((step % 2) * 256 + 128, 128), 128)] = both[128:256]

        @pl.loop(0, 4)
        def _(n):
            cols = pl.ds(pl.multiple_of(n * 1024, 1024), 1024)
            term = dot(mixed[...], proj[:, cols]).astype(BF)
            keep[i, :, cols] = term[0:128]
            give[i, :, cols] = term[128:256]

        to_sibling(i).start()

    left, right = slice(0, 2048), slice(2048, 4096)

    def pair(i, cols):
        return keep[i, :, cols].astype(F32) + sib[i, :, cols].astype(F32)

    partial(0)
    partial(1)
    to_sibling(0).wait_recv()
    relay_out[0] = pair(0, left).astype(BF)
    to_relay(0).start()
    relay_out[1] = pair(0, right).astype(BF)
    to_relay(1).start()
    partial(2)
    to_sibling(1).wait_recv()
    sums[0, :, right] = pair(1, right).astype(BF)
    to_relay(0).wait_recv()
    sums[0, :, left] = (pair(1, left) + relay_in[0].astype(F32)).astype(BF)
    to_owner(0).start()
    to_sibling(2).wait_recv()
    sums[1, :, left] = pair(2, left).astype(BF)
    to_relay(1).wait_recv()
    sums[1, :, right] = (pair(2, right) + relay_in[1].astype(F32)).astype(BF)
    to_owner(1).start()
    partial(3)
    to_sibling(3).wait_recv()
    for n in range(4):
        cols = slice(n * 1024, (n + 1) * 1024)
        hidden[:, cols] = residual[:, cols].astype(F32) + pair(3, cols)
    to_owner(0).wait_recv()
    to_owner(1).wait_recv()
    square = jnp.zeros((128, 1), F32)
    for n in range(4):
        cols = slice(n * 1024, (n + 1) * 1024)
        full = hidden[:, cols] + (land[0, :, cols].astype(F32) + land[1, :, cols].astype(F32))
        hidden[:, cols] = full
        square = square + jnp.sum(full * full, axis=-1, keepdims=True)
    factor = lax.rsqrt(square * (1.0 / 4096) + 1e-06)
    for n in range(4):
        cols = slice(n * 1024, (n + 1) * 1024)
        normed[:, cols] = (hidden[:, cols] * factor * gain[:, cols]).astype(BF)

    for s in range(1, 8):
        send_kv(s).wait_send()
        send_q(s).wait_send()
    for i in range(4):
        to_sibling(i).wait_send()
    for i in range(2):
        to_relay(i).wait_send()
        to_owner(i).wait_send()


def front(queries, keys, values, residual, out_proj, norm_gain):
    q_in = jnp.transpose(queries, (1, 0, 2)).reshape(8, 512, 128)
    kv_in = jnp.transpose(jnp.stack([keys, values]), (2, 0, 1, 3))
    vmem = pl.BlockSpec(memory_space=pltpu.VMEM)
    hbm = pl.BlockSpec(memory_space=pl.ANY)
    return pl.pallas_call(
        front_kernel,
        out_shape=(
            jax.ShapeDtypeStruct((128, 4096), F32),
            jax.ShapeDtypeStruct((128, 4096), BF),
        ),
        in_specs=[hbm, hbm, vmem, hbm, vmem],
        out_specs=(vmem, vmem),
        scratch_shapes=[
            pltpu.VMEM((8, 512, 128), BF),
            pltpu.VMEM((2, 1024, 128), BF),
            pltpu.VMEM((512, 4096), BF),
            pltpu.VMEM((256, 512), BF),
            pltpu.VMEM((4, 128, 4096), BF),
            pltpu.VMEM((4, 128, 4096), BF),
            pltpu.VMEM((4, 128, 4096), BF),
            pltpu.VMEM((2, 128, 2048), BF),
            pltpu.VMEM((2, 128, 2048), BF),
            pltpu.VMEM((2, 128, 4096), BF),
            pltpu.VMEM((2, 128, 4096), BF),
            pltpu.SemaphoreType.DMA((1,)),
            pltpu.SemaphoreType.DMA((8,)),
            pltpu.SemaphoreType.DMA((8,)),
            pltpu.SemaphoreType.DMA((8,)),
            pltpu.SemaphoreType.DMA((8,)),
            pltpu.SemaphoreType.DMA((4,)),
            pltpu.SemaphoreType.DMA((4,)),
            pltpu.SemaphoreType.DMA((2,)),
            pltpu.SemaphoreType.DMA((2,)),
            pltpu.SemaphoreType.DMA((2,)),
            pltpu.SemaphoreType.DMA((2,)),
        ],
        compiler_params=pltpu.CompilerParams(
            collective_id=0, has_side_effects=True, vmem_limit_bytes=48 * 2**20
        ),
        cost_estimate=pl.CostEstimate(
            flops=7_000_000_000, bytes_accessed=9_000_000, transcendentals=4_000_000
        ),
    )(q_in, kv_in, residual, out_proj, norm_gain.reshape(1, 4096))


def shards(
    queries,
    keys,
    values,
    residual,
    out_proj,
    norm_gain,
    expert_ids,
    gate_weights,
    w_gate,
    w_up,
    w_down,
):
    hidden, normed = front(queries, keys, values, residual, out_proj, norm_gain)
    return moe(normed, hidden, expert_ids, gate_weights, w_gate, w_up, w_down)


def solution(mesh):
    in_specs = (
        P(("wide", "narrow"), None, None),
        P(("wide", "narrow"), None, None),
        P(("wide", "narrow"), None, None),
        P(("wide", "narrow"), None),
        P("narrow", None),
        P(),
        P(("wide", "narrow"), None),
        P(("wide", "narrow"), None),
        P(("wide", "narrow"), None, None),
        P(("wide", "narrow"), None, None),
        P(("wide", "narrow"), None, None),
    )
    out_specs = P(("wide", "narrow"), None)
    return jax.shard_map(shards, mesh=mesh, in_specs=in_specs, out_specs=out_specs, check_vma=False)
```

```python
import math

import jax
import jax.numpy as jnp
from jax import lax
from jax.experimental import pallas as pl
from jax.experimental.pallas import tpu as pltpu
from jax.sharding import PartitionSpec as P

MESH = pl.DeviceIdType.MESH
BF = jnp.bfloat16
F32 = jnp.float32


def offset_of(k):
    j = (128 - k) & 127
    return j, (j >> 2) + j, (j >> 4) + (j >> 2) + j, j >> 6


def peer_of(k, sign):
    wide, narrow = lax.axis_index("wide"), lax.axis_index("narrow")
    dx, dy, dz, dc = offset_of(k)
    x = ((wide >> 2) + sign * dx) & 3
    y = (wide + sign * dy) & 3
    z = ((narrow >> 1) + sign * dz) & 3
    c = (narrow + dc) & 1
    return (x * 4 + y, z * 2 + c)


def iota2(shape, dim):
    return lax.broadcasted_iota(jnp.int32, shape, dim)


def dot(a, b):
    return jnp.dot(a, b, preferred_element_type=F32)


def block_kernel(
    q_in,
    kv_in,
    res_hbm,
    proj_hbm,
    gain,
    rank,
    rank_t,
    share_hi,
    share_lo,
    wg_hbm,
    wu_hbm,
    wd_hbm,
    out,
    stage,
    recv,
    ret,
    wg,
    wu,
    wd,
    n2,
    g8,
    rows,
    inner,
    acc,
    q_all,
    kv_all,
    mixed,
    row_in,
    w_sem,
    q_send,
    q_recv,
    kv_send,
    kv_recv,
    s_send,
    s_recv,
    y_send,
    y_recv,
    l_send,
    l_recv,
    d_send,
    d_recv,
    r_send,
    r_recv,
):
    wide, narrow = lax.axis_index("wide"), lax.axis_index("narrow")
    z, c = narrow >> 1, narrow & 1

    def at(dz, dc):
        return ((z + dz) & 3) * 2 + ((c + dc) & 1)

    barrier = pltpu.get_barrier_semaphore()
    for d in range(1, 8):
        pl.semaphore_signal(
            barrier, inc=1, device_id=(wide, (narrow + d) & 7), device_id_type=MESH
        )
    for d in range(1, 16):
        pl.semaphore_signal(
            barrier, inc=1, device_id=((wide + d) & 15, narrow), device_id_type=MESH
        )

    proj = wd.at[0:512, :]
    load_proj = pltpu.make_async_copy(proj_hbm, proj, w_sem.at[0])
    load_proj.start()
    load_res = [
        pltpu.make_async_copy(
            res_hbm.at[:, h * 2048 : (h + 1) * 2048],
            n2.at[h * 128 : (h + 1) * 128, :],
            w_sem.at[1 + h],
        )
        for h in range(2)
    ]
    for load in load_res:
        load.start()

    def mine(start):
        return pl.ds(pl.multiple_of(start * 128, 128), 128)

    def send_q(s):
        to = at(s // 2, s % 2)
        return pltpu.make_async_remote_copy(
            src_ref=q_in.at[to],
            dst_ref=q_all.at[narrow],
            send_sem=q_send.at[s],
            recv_sem=q_recv.at[s],
            device_id=(wide, to),
            device_id_type=MESH,
        )

    def send_kv(s):
        to = at(s // 2, s % 2)
        return pltpu.make_async_remote_copy(
            src_ref=kv_in.at[to // 2],
            dst_ref=kv_all.at[:, mine(narrow), :],
            send_sem=kv_send.at[s],
            recv_sem=kv_recv.at[s],
            device_id=(wide, to),
            device_id_type=MESH,
        )

    own_q = pltpu.make_async_copy(q_in.at[narrow], q_all.at[narrow], q_recv.at[0])
    own_kv = pltpu.make_async_copy(kv_in.at[z], kv_all.at[:, mine(narrow), :], kv_recv.at[0])
    own_q.start()
    own_kv.start()
    pl.semaphore_wait(barrier, 22)
    for s in (4, 5, 2, 6, 3, 7, 1):
        send_kv(s).start()
    for s in (4, 5, 2, 6, 3, 7, 1):
        send_q(s).start()
    for d in range(1, 8):
        pl.semaphore_signal(row_in, inc=1, device_id=(wide, (narrow + d) & 7), device_id_type=MESH)

    loads = [
        pltpu.make_async_copy(src.at[0], dst, w_sem.at[3 + i])
        for i, (src, dst) in enumerate(((wg_hbm, wg), (wu_hbm, wu), (wd_hbm, wd)))
    ]
    loads[0].start()
    loads[1].start()

    def folded_at(ref, i, half=None):
        if half is None:
            return ref.at[i * 256 : (i + 1) * 256, 0:2048]
        return ref.at[i * 256 + half * 128 : i * 256 + (half + 1) * 128, 0:2048]

    def remote(src, dst, sends, recvs, i, to):
        return pltpu.make_async_remote_copy(
            src_ref=src,
            dst_ref=dst,
            send_sem=sends.at[i],
            recv_sem=recvs.at[i],
            device_id=(wide, to),
            device_id_type=MESH,
        )

    def to_sibling(i):
        return remote(folded_at(stage, 4 + i), folded_at(ret, i), s_send, s_recv, i, at(0, 1))

    def to_relay(i):
        return remote(
            folded_at(stage, 0, i), folded_at(ret, 6, i), y_send, y_recv, i, at((1, 3)[i], 0)
        )

    def to_owner(i):
        return remote(
            folded_at(stage, 1 + i), folded_at(ret, 4 + i), l_send, l_recv, i, at((1, 3)[i], 0)
        )

    own_kv.wait()
    for s in range(1, 8):
        send_kv(s).wait_recv()
    load_proj.wait()

    scale = math.log2(math.e) / math.sqrt(128)
    q_row, k_col = iota2((256, 1024), 0) & 127, iota2((256, 1024), 1)

    def partial(i):
        dz = (2, 1, 3, 0)[i]
        back = (4 - dz) % 4
        for s in (back * 2, back * 2 + 1):
            if s == 0:
                own_q.wait()
            else:
                send_q(s).wait_recv()

        @pl.loop(0, 4)
        def _(step):
            block = at(dz, step // 2)
            part = pl.ds(pl.multiple_of((step % 2) * 256, 256), 256)
            query = q_all[block, part, :]
            scores = lax.dot_general(
                query, kv_all[0], (((1,), (1,)), ((), ())), preferred_element_type=F32
            )
            scores = jnp.where(q_row + block * 128 >= k_col, scores, -1e30)
            highest = jnp.max(scores, axis=-1, keepdims=True)
            weights = jnp.exp2((scores - highest) * scale)
            total = jnp.sum(weights, axis=-1, keepdims=True)
            both = (dot(weights.astype(BF), kv_all[1]) / total).astype(BF)
            down = mine(step // 2)
            mixed[down, pl.ds(pl.multiple_of((step % 2) * 256, 256), 128)] = both[0:128]
            mixed[down, pl.ds(pl.multiple_of((step % 2) * 256 + 128, 128), 128)] = both[128:256]

        @pl.loop(0, 4)
        def _(n):
            cols = pl.ds(pl.multiple_of(n * 1024, 1024), 1024)
            inside = pl.ds(pl.multiple_of((n % 2) * 1024, 1024), 1024)
            term = dot(mixed[...], wd[0:512, cols]).astype(BF)
            stage[pl.ds(pl.multiple_of(i * 256 + (n // 2) * 128, 128), 128), inside] = term[0:128]
            stage[pl.ds(pl.multiple_of(i * 256 + 1024 + (n // 2) * 128, 128), 128), inside] = term[
                128:256
            ]

        to_sibling(i).start()

    def pair(i, half):
        return folded_at(stage, i, half)[...].astype(F32) + folded_at(ret, i, half)[...].astype(F32)

    def passed_on(i):
        return folded_at(ret, 6, i)[...].astype(F32)

    partial(0)
    partial(1)
    to_sibling(0).wait_recv()
    for h in range(2):
        folded_at(stage, 0, h)[...] = pair(0, h).astype(BF)
        to_relay(h).start()
    partial(2)
    to_sibling(1).wait_recv()
    folded_at(stage, 1, 1)[...] = pair(1, 1).astype(BF)
    to_relay(0).wait_recv()
    folded_at(stage, 1, 0)[...] = (pair(1, 0) + passed_on(0)).astype(BF)
    to_owner(0).start()
    to_sibling(2).wait_recv()
    folded_at(stage, 2, 0)[...] = pair(2, 0).astype(BF)
    to_relay(1).wait_recv()
    folded_at(stage, 2, 1)[...] = (pair(2, 1) + passed_on(1)).astype(BF)
    to_owner(1).start()
    partial(3)
    loads[2].start()
    for load in load_res:
        load.wait()
    to_sibling(3).wait_recv()
    for h in range(2):
        half = slice(h * 128, (h + 1) * 128)
        acc[half, :] = n2[half, :].astype(F32) + pair(3, h)
    to_owner(0).wait_recv()
    to_owner(1).wait_recv()
    square = jnp.zeros((128, 1), F32)
    for h in range(2):
        half = slice(h * 128, (h + 1) * 128)
        full = acc[half, :] + (
            folded_at(ret, 4, h)[...].astype(F32) + folded_at(ret, 5, h)[...].astype(F32)
        )
        acc[half, :] = full
        square = square + jnp.sum(full * full, axis=-1, keepdims=True)
    factor = lax.rsqrt(square * (1.0 / 4096) + 1e-06)
    for h in range(2):
        half = slice(h * 128, (h + 1) * 128)
        n2[half, :] = (acc[half, :] * factor * gain[:, h * 2048 : (h + 1) * 2048]).astype(BF)

    for s in range(1, 8):
        send_kv(s).wait_send()
        send_q(s).wait_send()
    for i in range(4):
        to_sibling(i).wait_send()
    for i in range(2):
        to_relay(i).wait_send()
        to_owner(i).wait_send()

    to_row = iota2((256, 256), 0)
    to_col = iota2((256, 256), 1)

    def folded(i):
        return ((i >> 3) & 15) * 16 + (i >> 7) * 8 + (i & 7)

    def ones_where(mask):
        return jnp.where(mask, 1.0, 0.0).astype(BF)

    unfold = ones_where(to_col == folded(to_row))
    fold = ones_where(to_row == folded(to_col))
    swap = ones_where(to_col == (to_row & 15) * 16 + (to_row >> 4))

    def slab(k):
        return pl.ds(pl.multiple_of(k * 16, 16), 16)

    def group(q):
        return pl.ds(pl.multiple_of(q * 256, 256), 256)

    def dispatch(k):
        return pltpu.make_async_remote_copy(
            src_ref=stage.at[slab(k)],
            dst_ref=recv.at[slab(k)],
            send_sem=d_send.at[k],
            recv_sem=d_recv.at[k],
            device_id=peer_of(k, 1),
            device_id_type=MESH,
        )

    def give_back(k):
        return pltpu.make_async_remote_copy(
            src_ref=recv.at[slab(k)],
            dst_ref=ret.at[slab(k)],
            send_sem=r_send.at[k],
            recv_sem=r_recv.at[k],
            device_id=peer_of(k, -1),
            device_id_type=MESH,
        )

    own_in = pltpu.make_async_copy(stage.at[pl.ds(0, 16)], recv.at[pl.ds(0, 16)], d_recv.at[0])
    own_out = pltpu.make_async_copy(recv.at[pl.ds(0, 16)], ret.at[pl.ds(0, 16)], r_recv.at[0])

    pick8 = ones_where(rank_t[...] == 8.0)

    for n in range(4):
        half, inside = n // 2, slice((n % 2) * 1024, (n % 2 + 1) * 1024)
        g8[:, n * 1024 : (n + 1) * 1024] = dot(
            pick8, n2[half * 128 : (half + 1) * 128, inside]
        ).astype(BF)

    spread_row, spread_col = iota2((256, 128), 0), iota2((256, 128), 1)
    slot_row = (spread_row & 7).astype(F32)
    low_row = (spread_row & 8) == 0

    pl.semaphore_wait(row_in, 7)

    @pl.loop(0, 8)
    def _(q):
        spread = ones_where((spread_row >> 4) + q * 16 == spread_col)
        hit = dot(spread, rank_t[...].astype(BF)) == slot_row
        pick = jnp.concatenate(
            [ones_where(hit & low_row), ones_where(hit & jnp.logical_not(low_row))], axis=1
        )
        for n in range(4):
            stage[group(q), n * 512 : (n + 1) * 512] = dot(
                pick, n2[:, n * 512 : (n + 1) * 512]
            ).astype(BF)
        some = g8[slab(q), :]
        piled = jnp.concatenate([some[:, g * 256 : (g + 1) * 256] for g in range(16)], axis=0)
        stage[group(q), 2048:2304] = dot(swap, piled).astype(BF)

        @pl.loop(0, 16)
        def _(i):
            k = q * 16 + i

            @pl.when(k > 0)
            def _():
                dispatch(k).start()

    own_in.start()
    for load in loads:
        load.wait()

    @pl.loop(0, 4)
    def _(j):
        @pl.loop(0, 32)
        def _(i):
            k = j * 32 + i

            @pl.when(k > 0)
            def _():
                dispatch(k).wait_recv()

            @pl.when(k == 0)
            def _():
                own_in.wait()

        for q in range(2):
            part = group(j * 2 + q)
            for n in range(4):
                cols = slice(n * 512, (n + 1) * 512)
                wide_rows = dot(unfold, recv[part, cols]).astype(BF)
                rows[q * 128 : (q + 1) * 128, n * 512 : (n + 1) * 512] = wide_rows[0:128]
                rows[q * 128 : (q + 1) * 128, 2048 + n * 512 : 2048 + (n + 1) * 512] = wide_rows[
                    128:256
                ]
            last = dot(swap, recv[part, 2048:2304]).astype(BF)
            for g in range(16):
                rows[256 + q * 16 : 272 + q * 16, g * 256 : (g + 1) * 256] = last[
                    g * 16 : (g + 1) * 16
                ]

        @pl.loop(0, 3)
        def _(n):
            cols = pl.ds(pl.multiple_of(n * 256, 256), 256)
            gated = dot(rows[...], wg[:, cols])
            upward = dot(rows[...], wu[:, cols])
            inner[:, cols] = (gated / (1.0 + jnp.exp(-gated)) * upward).astype(BF)

        @pl.loop(0, 8)
        def _(n):
            cols = pl.ds(pl.multiple_of(n * 512, 512), 512)
            rows[:, cols] = dot(inner[...], wd[:, cols]).astype(BF)

        for q in range(2):
            part = group(j * 2 + q)
            for n in range(4):
                piled = jnp.concatenate(
                    [
                        rows[q * 128 : (q + 1) * 128, n * 512 : (n + 1) * 512],
                        rows[q * 128 : (q + 1) * 128, 2048 + n * 512 : 2048 + (n + 1) * 512],
                    ],
                    axis=0,
                )
                recv[part, n * 512 : (n + 1) * 512] = dot(fold, piled).astype(BF)
            piled = jnp.concatenate(
                [
                    rows[256 + q * 16 : 272 + q * 16, g * 256 : (g + 1) * 256]
                    for g in range(16)
                ],
                axis=0,
            )
            recv[part, 2048:2304] = dot(swap, piled).astype(BF)

        @pl.loop(0, 32)
        def _(i):
            k = j * 32 + i

            @pl.when(k > 0)
            def _():
                give_back(k).start()

            @pl.when(k == 0)
            def _():
                own_out.start()

    lane_row, lane_col = iota2((128, 256), 0), iota2((128, 256), 1)
    slot_col = (lane_col & 7).astype(F32)
    low_col = (lane_col & 8) == 0

    @pl.loop(0, 8)
    def _(q):
        @pl.loop(0, 16)
        def _(i):
            k = q * 16 + i

            @pl.when(k > 0)
            def _():
                give_back(k).wait_recv()

            @pl.when(k == 0)
            def _():
                own_out.wait()

        spread = ones_where((lane_col >> 4) + q * 16 == lane_row)
        hit = dot(rank[...].astype(BF), spread) == slot_col
        high = jnp.where(hit, dot(share_hi[...], spread), 0.0)
        low = jnp.where(hit, dot(share_lo[...], spread), 0.0)

        def both(a):
            return jnp.concatenate(
                [jnp.where(low_col, a, 0.0), jnp.where(low_col, 0.0, a)], axis=0
            ).astype(BF)

        mix_hi, mix_lo = both(high), both(low)
        for n in range(4):
            cols = slice(n * 512, (n + 1) * 512)
            block = ret[group(q), cols]
            acc[:, cols] += dot(mix_hi, block) + dot(mix_lo, block)
        last = dot(swap, ret[group(q), 2048:2304]).astype(BF)
        for g in range(16):
            g8[slab(q), g * 256 : (g + 1) * 256] = last[g * 16 : (g + 1) * 16]

    at_last = rank[...] == 8.0
    mix8_hi = jnp.where(at_last, share_hi[...].astype(F32), 0.0).astype(BF)
    mix8_lo = jnp.where(at_last, share_lo[...].astype(F32), 0.0).astype(BF)
    for n in range(8):
        cols = slice(n * 512, (n + 1) * 512)
        half, inside = n // 4, slice((n % 4) * 512, (n % 4 + 1) * 512)
        block = g8[:, cols]
        total = acc[half * 128 : (half + 1) * 128, inside]
        total = total + dot(mix8_hi, block) + dot(mix8_lo, block)
        out[:, cols] = total.astype(BF)

    @pl.loop(1, 128)
    def _(k):
        dispatch(k).wait_send()
        give_back(k).wait_send()


def shards(
    queries,
    keys,
    values,
    residual,
    out_proj,
    norm_gain,
    expert_ids,
    gate_weights,
    w_gate,
    w_up,
    w_down,
):
    q_in = jnp.transpose(queries, (1, 0, 2)).reshape(8, 512, 128)
    kv_in = jnp.transpose(jnp.stack([keys, values]), (2, 0, 1, 3))
    steps = jnp.arange(128, dtype=jnp.int32)
    wide, narrow = peer_of(steps, 1)
    expert_at = wide * 8 + narrow
    named = expert_ids[:, :, None] == expert_at[None, None, :]
    chosen = jnp.any(named, axis=1)
    share = jnp.sum(jnp.where(named, gate_weights[:, :, None], 0.0), axis=1)
    before = iota2((128, 128), 0) > iota2((128, 128), 1)
    rank = jnp.where(chosen, dot(before.astype(BF), chosen.astype(BF)), -1.0)
    share_hi = share.astype(BF)
    share_lo = (share - share_hi.astype(F32)).astype(BF)

    vmem = pl.BlockSpec(memory_space=pltpu.VMEM)
    hbm = pl.BlockSpec(memory_space=pl.ANY)
    return pl.pallas_call(
        block_kernel,
        out_shape=jax.ShapeDtypeStruct((128, 4096), BF),
        in_specs=[hbm] * 4 + [vmem] * 5 + [hbm] * 3,
        out_specs=vmem,
        scratch_shapes=[
            pltpu.VMEM((2048, 2304), BF),
            pltpu.VMEM((2048, 2304), BF),
            pltpu.VMEM((2048, 2304), BF),
            pltpu.VMEM((4096, 768), BF),
            pltpu.VMEM((4096, 768), BF),
            pltpu.VMEM((768, 4096), BF),
            pltpu.VMEM((256, 2048), BF),
            pltpu.VMEM((128, 4096), BF),
            pltpu.VMEM((288, 4096), BF),
            pltpu.VMEM((288, 768), BF),
            pltpu.VMEM((256, 2048), F32),
            pltpu.VMEM((8, 512, 128), BF),
            pltpu.VMEM((2, 1024, 128), BF),
            pltpu.VMEM((256, 512), BF),
            pltpu.SemaphoreType.REGULAR,
            pltpu.SemaphoreType.DMA((6,)),
            pltpu.SemaphoreType.DMA((8,)),
            pltpu.SemaphoreType.DMA((8,)),
            pltpu.SemaphoreType.DMA((8,)),
            pltpu.SemaphoreType.DMA((8,)),
            pltpu.SemaphoreType.DMA((4,)),
            pltpu.SemaphoreType.DMA((4,)),
            pltpu.SemaphoreType.DMA((2,)),
            pltpu.SemaphoreType.DMA((2,)),
            pltpu.SemaphoreType.DMA((2,)),
            pltpu.SemaphoreType.DMA((2,)),
            pltpu.SemaphoreType.DMA((128,)),
            pltpu.SemaphoreType.DMA((128,)),
            pltpu.SemaphoreType.DMA((128,)),
            pltpu.SemaphoreType.DMA((128,)),
        ],
        compiler_params=pltpu.CompilerParams(
            collective_id=1, has_side_effects=True, vmem_limit_bytes=62 * 2**20
        ),
        cost_estimate=pl.CostEstimate(
            flops=32_000_000_000, bytes_accessed=30_000_000, transcendentals=5_000_000
        ),
    )(
        q_in,
        kv_in,
        residual,
        out_proj,
        norm_gain.reshape(1, 4096),
        rank,
        rank.T,
        share_hi,
        share_lo,
        w_gate,
        w_up,
        w_down,
    )


def solution(mesh):
    in_specs = (
        P(("wide", "narrow"), None, None),
        P(("wide", "narrow"), None, None),
        P(("wide", "narrow"), None, None),
        P(("wide", "narrow"), None),
        P("narrow", None),
        P(),
        P(("wide", "narrow"), None),
        P(("wide", "narrow"), None),
        P(("wide", "narrow"), None, None),
        P(("wide", "narrow"), None, None),
        P(("wide", "narrow"), None, None),
    )
    out_specs = P(("wide", "narrow"), None)
    return jax.shard_map(shards, mesh=mesh, in_specs=in_specs, out_specs=out_specs, check_vma=False)
```

```python
import math

import jax
import jax.numpy as jnp
from jax import lax
from jax.experimental import pallas as pl
from jax.experimental.pallas import tpu as pltpu
from jax.sharding import PartitionSpec as P

MESH = pl.DeviceIdType.MESH
BF = jnp.bfloat16
F32 = jnp.float32


def offset_of(k):
    j = (128 - k) & 127
    return j, (j >> 2) + j, (j >> 4) + (j >> 2) + j, j >> 6


def peer_of(k, sign):
    wide, narrow = lax.axis_index("wide"), lax.axis_index("narrow")
    dx, dy, dz, dc = offset_of(k)
    x = ((wide >> 2) + sign * dx) & 3
    y = (wide + sign * dy) & 3
    z = ((narrow >> 1) + sign * dz) & 3
    c = (narrow + dc) & 1
    return (x * 4 + y, z * 2 + c)


def iota2(shape, dim):
    return lax.broadcasted_iota(jnp.int32, shape, dim)


def dot(a, b):
    return jnp.dot(a, b, preferred_element_type=F32)


def block_kernel(
    q_in,
    kv_in,
    res_hbm,
    proj_hbm,
    gain,
    ids,
    gates,
    wg_hbm,
    wu_hbm,
    wd_hbm,
    out,
    stage,
    recv,
    ret,
    wg,
    wu,
    wd,
    n2,
    g8,
    rows,
    inner,
    acc,
    q_all,
    kv_all,
    mixed,
    rank,
    rank_t,
    share_hi,
    share_lo,
    row_in,
    w_sem,
    q_send,
    q_recv,
    kv_send,
    kv_recv,
    s_send,
    s_recv,
    y_send,
    y_recv,
    l_send,
    l_recv,
    d_send,
    d_recv,
    r_send,
    r_recv,
):
    wide, narrow = lax.axis_index("wide"), lax.axis_index("narrow")
    z, c = narrow >> 1, narrow & 1

    def at(dz, dc):
        return ((z + dz) & 3) * 2 + ((c + dc) & 1)

    barrier = pltpu.get_barrier_semaphore()
    for d in range(1, 8):
        pl.semaphore_signal(
            barrier, inc=1, device_id=(wide, (narrow + d) & 7), device_id_type=MESH
        )
    for d in range(1, 16):
        pl.semaphore_signal(
            barrier, inc=1, device_id=((wide + d) & 15, narrow), device_id_type=MESH
        )

    proj = wd.at[0:512, :]
    load_proj = pltpu.make_async_copy(proj_hbm, proj, w_sem.at[0])
    load_proj.start()
    load_res = [
        pltpu.make_async_copy(
            res_hbm.at[:, h * 2048 : (h + 1) * 2048],
            n2.at[h * 128 : (h + 1) * 128, :],
            w_sem.at[1 + h],
        )
        for h in range(2)
    ]
    for load in load_res:
        load.start()

    def mine(start):
        return pl.ds(pl.multiple_of(start * 128, 128), 128)

    def send_q(s):
        to = at(s // 2, s % 2)
        return pltpu.make_async_remote_copy(
            src_ref=q_in.at[to],
            dst_ref=q_all.at[narrow],
            send_sem=q_send.at[s],
            recv_sem=q_recv.at[s],
            device_id=(wide, to),
            device_id_type=MESH,
        )

    def send_kv(s):
        to = at(s // 2, s % 2)
        return pltpu.make_async_remote_copy(
            src_ref=kv_in.at[to // 2],
            dst_ref=kv_all.at[:, mine(narrow), :],
            send_sem=kv_send.at[s],
            recv_sem=kv_recv.at[s],
            device_id=(wide, to),
            device_id_type=MESH,
        )

    own_q = pltpu.make_async_copy(q_in.at[narrow], q_all.at[narrow], q_recv.at[0])
    own_kv = pltpu.make_async_copy(kv_in.at[z], kv_all.at[:, mine(narrow), :], kv_recv.at[0])
    own_q.start()
    own_kv.start()
    pl.semaphore_wait(barrier, 22)
    for s in (4, 5, 2, 6, 3, 7, 1):
        send_kv(s).start()
    for s in (4, 5, 1):
        send_q(s).start()
    for d in range(1, 8):
        pl.semaphore_signal(row_in, inc=1, device_id=(wide, (narrow + d) & 7), device_id_type=MESH)

    loads = [
        pltpu.make_async_copy(src.at[0], dst, w_sem.at[3 + i])
        for i, (src, dst) in enumerate(((wg_hbm, wg), (wu_hbm, wu), (wd_hbm, wd)))
    ]
    loads[0].start()
    loads[1].start()

    def folded_at(ref, i, half=None):
        if half is None:
            return ref.at[i * 256 : (i + 1) * 256, 0:2048]
        return ref.at[i * 256 + half * 128 : i * 256 + (half + 1) * 128, 0:2048]

    def remote(src, dst, sends, recvs, i, to):
        return pltpu.make_async_remote_copy(
            src_ref=src,
            dst_ref=dst,
            send_sem=sends.at[i],
            recv_sem=recvs.at[i],
            device_id=(wide, to),
            device_id_type=MESH,
        )

    def to_sibling(i):
        return remote(folded_at(stage, 4 + i), folded_at(ret, i), s_send, s_recv, i, at(0, 1))

    def to_relay(i):
        return remote(
            folded_at(stage, 0, i), folded_at(ret, 6, i), y_send, y_recv, i, at((1, 3)[i], 0)
        )

    def to_owner(i):
        return remote(
            folded_at(stage, 1 + i), folded_at(ret, 4 + i), l_send, l_recv, i, at((1, 3)[i], 0)
        )

    wide_at, narrow_at = peer_of(iota2((128, 128), 1), 1)
    expert_at = wide_at * 8 + narrow_at
    chosen = jnp.zeros((128, 128), F32)
    share = jnp.zeros((128, 128), F32)
    for i in range(8):
        named = ids[:, i : i + 1] == expert_at
        chosen = jnp.where(named, 1.0, chosen)
        share = jnp.where(named, gates[:, i : i + 1], share)
    tri_row, tri_col = iota2((128, 128), 0), iota2((128, 128), 1)
    before = jnp.where(tri_row > tri_col, 1.0, 0.0).astype(BF)
    same = jnp.where(tri_row == tri_col, 1.0, 0.0).astype(BF)
    ranked = jnp.where(chosen > 0.5, dot(before, chosen.astype(BF)), -1.0)
    rank[...] = ranked
    rank_t[...] = lax.dot_general(
        same, ranked.astype(BF), (((1,), (1,)), ((), ())), preferred_element_type=F32
    )
    share_hi[...] = share.astype(BF)
    share_lo[...] = (share - share.astype(BF).astype(F32)).astype(BF)

    own_kv.wait()
    for s in range(1, 8):
        send_kv(s).wait_recv()
    for s in (6, 7, 2, 3):
        send_q(s).start()
    load_proj.wait()

    scale = math.log2(math.e) / math.sqrt(128)
    q_row, k_col = iota2((256, 1024), 0) & 127, iota2((256, 1024), 1)

    def partial(i):
        dz = (2, 1, 3, 0)[i]
        back = (4 - dz) % 4
        for s in (back * 2, back * 2 + 1):
            if s == 0:
                own_q.wait()
            else:
                send_q(s).wait_recv()

        @pl.loop(0, 4)
        def _(step):
            block = at(dz, step // 2)
            part = pl.ds(pl.multiple_of((step % 2) * 256, 256), 256)
            query = q_all[block, part, :]
            scores = lax.dot_general(
                query, kv_all[0], (((1,), (1,)), ((), ())), preferred_element_type=F32
            )
            scores = jnp.where(q_row + block * 128 >= k_col, scores, -1e30)
            highest = jnp.max(scores, axis=-1, keepdims=True)
            weights = jnp.exp2((scores - highest) * scale)
            total = jnp.sum(weights, axis=-1, keepdims=True)
            both = (dot(weights.astype(BF), kv_all[1]) / total).astype(BF)
            down = mine(step // 2)
            mixed[down, pl.ds(pl.multiple_of((step % 2) * 256, 256), 128)] = both[0:128]
            mixed[down, pl.ds(pl.multiple_of((step % 2) * 256 + 128, 128), 128)] = both[128:256]

        @pl.loop(0, 4)
        def _(n):
            cols = pl.ds(pl.multiple_of(n * 1024, 1024), 1024)
            inside = pl.ds(pl.multiple_of((n % 2) * 1024, 1024), 1024)
            term = dot(mixed[...], wd[0:512, cols]).astype(BF)
            stage[pl.ds(pl.multiple_of(i * 256 + (n // 2) * 128, 128), 128), inside] = term[0:128]
            stage[pl.ds(pl.multiple_of(i * 256 + 1024 + (n // 2) * 128, 128), 128), inside] = term[
                128:256
            ]

        to_sibling(i).start()

    def pair(i, half):
        return folded_at(stage, i, half)[...].astype(F32) + folded_at(ret, i, half)[...].astype(F32)

    def passed_on(i):
        return folded_at(ret, 6, i)[...].astype(F32)

    partial(0)
    partial(1)
    to_sibling(0).wait_recv()
    for h in range(2):
        folded_at(stage, 0, h)[...] = pair(0, h).astype(BF)
        to_relay(h).start()
    partial(2)
    to_sibling(1).wait_recv()
    folded_at(stage, 1, 1)[...] = pair(1, 1).astype(BF)
    to_relay(0).wait_recv()
    folded_at(stage, 1, 0)[...] = (pair(1, 0) + passed_on(0)).astype(BF)
    to_owner(0).start()
    to_sibling(2).wait_recv()
    folded_at(stage, 2, 0)[...] = pair(2, 0).astype(BF)
    to_relay(1).wait_recv()
    folded_at(stage, 2, 1)[...] = (pair(2, 1) + passed_on(1)).astype(BF)
    to_owner(1).start()
    partial(3)
    loads[2].start()
    for load in load_res:
        load.wait()
    to_sibling(3).wait_recv()
    for h in range(2):
        half = slice(h * 128, (h + 1) * 128)
        acc[half, :] = n2[half, :].astype(F32) + pair(3, h)
    to_owner(0).wait_recv()
    to_owner(1).wait_recv()
    square = jnp.zeros((128, 1), F32)
    for h in range(2):
        half = slice(h * 128, (h + 1) * 128)
        full = acc[half, :] + (
            folded_at(ret, 4, h)[...].astype(F32) + folded_at(ret, 5, h)[...].astype(F32)
        )
        acc[half, :] = full
        square = square + jnp.sum(full * full, axis=-1, keepdims=True)
    factor = lax.rsqrt(square * (1.0 / 4096) + 1e-06)
    for h in range(2):
        half = slice(h * 128, (h + 1) * 128)
        n2[half, :] = (acc[half, :] * factor * gain[:, h * 2048 : (h + 1) * 2048]).astype(BF)

    for s in range(1, 8):
        send_kv(s).wait_send()
        send_q(s).wait_send()
    for i in range(4):
        to_sibling(i).wait_send()
    for i in range(2):
        to_relay(i).wait_send()
        to_owner(i).wait_send()

    to_row = iota2((256, 256), 0)
    to_col = iota2((256, 256), 1)

    def folded(i):
        return ((i >> 3) & 15) * 16 + (i >> 7) * 8 + (i & 7)

    def ones_where(mask):
        return jnp.where(mask, 1.0, 0.0).astype(BF)

    unfold = ones_where(to_col == folded(to_row))
    fold = ones_where(to_row == folded(to_col))
    swap = ones_where(to_col == (to_row & 15) * 16 + (to_row >> 4))

    def slab(k):
        return pl.ds(pl.multiple_of(k * 16, 16), 16)

    def group(q):
        return pl.ds(pl.multiple_of(q * 256, 256), 256)

    def dispatch(k):
        return pltpu.make_async_remote_copy(
            src_ref=stage.at[slab(k)],
            dst_ref=recv.at[slab(k)],
            send_sem=d_send.at[k],
            recv_sem=d_recv.at[k],
            device_id=peer_of(k, 1),
            device_id_type=MESH,
        )

    def give_back(k):
        return pltpu.make_async_remote_copy(
            src_ref=recv.at[slab(k)],
            dst_ref=ret.at[slab(k)],
            send_sem=r_send.at[k],
            recv_sem=r_recv.at[k],
            device_id=peer_of(k, -1),
            device_id_type=MESH,
        )

    own_in = pltpu.make_async_copy(stage.at[pl.ds(0, 16)], recv.at[pl.ds(0, 16)], d_recv.at[0])
    own_out = pltpu.make_async_copy(recv.at[pl.ds(0, 16)], ret.at[pl.ds(0, 16)], r_recv.at[0])

    pick8 = ones_where(rank_t[...] == 8.0)

    for n in range(4):
        half, inside = n // 2, slice((n % 2) * 1024, (n % 2 + 1) * 1024)
        g8[:, n * 1024 : (n + 1) * 1024] = dot(
            pick8, n2[half * 128 : (half + 1) * 128, inside]
        ).astype(BF)

    spread_row, spread_col = iota2((256, 128), 0), iota2((256, 128), 1)
    slot_row = (spread_row & 7).astype(F32)
    low_row = (spread_row & 8) == 0

    pl.semaphore_wait(row_in, 7)

    @pl.loop(0, 8)
    def _(q):
        spread = ones_where((spread_row >> 4) + q * 16 == spread_col)
        hit = dot(spread, rank_t[...].astype(BF)) == slot_row
        pick = jnp.concatenate(
            [ones_where(hit & low_row), ones_where(hit & jnp.logical_not(low_row))], axis=1
        )
        for n in range(4):
            stage[group(q), n * 512 : (n + 1) * 512] = dot(
                pick, n2[:, n * 512 : (n + 1) * 512]
            ).astype(BF)
        some = g8[slab(q), :]
        piled = jnp.concatenate([some[:, g * 256 : (g + 1) * 256] for g in range(16)], axis=0)
        stage[group(q), 2048:2304] = dot(swap, piled).astype(BF)

        @pl.loop(0, 16)
        def _(i):
            k = q * 16 + i

            @pl.when(k > 0)
            def _():
                dispatch(k).start()

    own_in.start()
    for load in loads:
        load.wait()

    @pl.loop(0, 4)
    def _(j):
        @pl.loop(0, 32)
        def _(i):
            k = j * 32 + i

            @pl.when(k > 0)
            def _():
                dispatch(k).wait_recv()

            @pl.when(k == 0)
            def _():
                own_in.wait()

        for q in range(2):
            part = group(j * 2 + q)
            for n in range(4):
                cols = slice(n * 512, (n + 1) * 512)
                wide_rows = dot(unfold, recv[part, cols]).astype(BF)
                rows[q * 128 : (q + 1) * 128, n * 512 : (n + 1) * 512] = wide_rows[0:128]
                rows[q * 128 : (q + 1) * 128, 2048 + n * 512 : 2048 + (n + 1) * 512] = wide_rows[
                    128:256
                ]
            last = dot(swap, recv[part, 2048:2304]).astype(BF)
            for g in range(16):
                rows[256 + q * 16 : 272 + q * 16, g * 256 : (g + 1) * 256] = last[
                    g * 16 : (g + 1) * 16
                ]

        @pl.loop(0, 3)
        def _(n):
            cols = pl.ds(pl.multiple_of(n * 256, 256), 256)
            gated = dot(rows[...], wg[:, cols])
            upward = dot(rows[...], wu[:, cols])
            inner[:, cols] = (gated / (1.0 + jnp.exp(-gated)) * upward).astype(BF)

        @pl.loop(0, 8)
        def _(n):
            cols = pl.ds(pl.multiple_of(n * 512, 512), 512)
            rows[:, cols] = dot(inner[...], wd[:, cols]).astype(BF)

        for q in range(2):
            part = group(j * 2 + q)
            for n in range(4):
                piled = jnp.concatenate(
                    [
                        rows[q * 128 : (q + 1) * 128, n * 512 : (n + 1) * 512],
                        rows[q * 128 : (q + 1) * 128, 2048 + n * 512 : 2048 + (n + 1) * 512],
                    ],
                    axis=0,
                )
                recv[part, n * 512 : (n + 1) * 512] = dot(fold, piled).astype(BF)
            piled = jnp.concatenate(
                [
                    rows[256 + q * 16 : 272 + q * 16, g * 256 : (g + 1) * 256]
                    for g in range(16)
                ],
                axis=0,
            )
            recv[part, 2048:2304] = dot(swap, piled).astype(BF)

        @pl.loop(0, 32)
        def _(i):
            k = j * 32 + i

            @pl.when(k > 0)
            def _():
                give_back(k).start()

            @pl.when(k == 0)
            def _():
                own_out.start()

    lane_row, lane_col = iota2((128, 256), 0), iota2((128, 256), 1)
    slot_col = (lane_col & 7).astype(F32)
    low_col = (lane_col & 8) == 0

    @pl.loop(0, 8)
    def _(q):
        @pl.loop(0, 16)
        def _(i):
            k = q * 16 + i

            @pl.when(k > 0)
            def _():
                give_back(k).wait_recv()

            @pl.when(k == 0)
            def _():
                own_out.wait()

        spread = ones_where((lane_col >> 4) + q * 16 == lane_row)
        hit = dot(rank[...].astype(BF), spread) == slot_col
        high = jnp.where(hit, dot(share_hi[...], spread), 0.0)
        low = jnp.where(hit, dot(share_lo[...], spread), 0.0)

        def both(a):
            return jnp.concatenate(
                [jnp.where(low_col, a, 0.0), jnp.where(low_col, 0.0, a)], axis=0
            ).astype(BF)

        mix_hi, mix_lo = both(high), both(low)
        for n in range(4):
            cols = slice(n * 512, (n + 1) * 512)
            block = ret[group(q), cols]
            acc[:, cols] += dot(mix_hi, block) + dot(mix_lo, block)
        last = dot(swap, ret[group(q), 2048:2304]).astype(BF)
        for g in range(16):
            g8[slab(q), g * 256 : (g + 1) * 256] = last[g * 16 : (g + 1) * 16]

    at_last = rank[...] == 8.0
    mix8_hi = jnp.where(at_last, share_hi[...].astype(F32), 0.0).astype(BF)
    mix8_lo = jnp.where(at_last, share_lo[...].astype(F32), 0.0).astype(BF)
    for n in range(8):
        cols = slice(n * 512, (n + 1) * 512)
        half, inside = n // 4, slice((n % 4) * 512, (n % 4 + 1) * 512)
        block = g8[:, cols]
        total = acc[half * 128 : (half + 1) * 128, inside]
        total = total + dot(mix8_hi, block) + dot(mix8_lo, block)
        out[:, cols] = total.astype(BF)

    @pl.loop(1, 128)
    def _(k):
        dispatch(k).wait_send()
        give_back(k).wait_send()


def shards(
    queries,
    keys,
    values,
    residual,
    out_proj,
    norm_gain,
    expert_ids,
    gate_weights,
    w_gate,
    w_up,
    w_down,
):
    q_in = jnp.transpose(queries, (1, 0, 2)).reshape(8, 512, 128)
    kv_in = jnp.transpose(jnp.stack([keys, values]), (2, 0, 1, 3))
    vmem = pl.BlockSpec(memory_space=pltpu.VMEM)
    hbm = pl.BlockSpec(memory_space=pl.ANY)
    return pl.pallas_call(
        block_kernel,
        out_shape=jax.ShapeDtypeStruct((128, 4096), BF),
        in_specs=[hbm] * 4 + [vmem] * 3 + [hbm] * 3,
        out_specs=vmem,
        scratch_shapes=[
            pltpu.VMEM((2048, 2304), BF),
            pltpu.VMEM((2048, 2304), BF),
            pltpu.VMEM((2048, 2304), BF),
            pltpu.VMEM((4096, 768), BF),
            pltpu.VMEM((4096, 768), BF),
            pltpu.VMEM((768, 4096), BF),
            pltpu.VMEM((256, 2048), BF),
            pltpu.VMEM((128, 4096), BF),
            pltpu.VMEM((288, 4096), BF),
            pltpu.VMEM((288, 768), BF),
            pltpu.VMEM((256, 2048), F32),
            pltpu.VMEM((8, 512, 128), BF),
            pltpu.VMEM((2, 1024, 128), BF),
            pltpu.VMEM((256, 512), BF),
            pltpu.VMEM((128, 128), F32),
            pltpu.VMEM((128, 128), F32),
            pltpu.VMEM((128, 128), BF),
            pltpu.VMEM((128, 128), BF),
            pltpu.SemaphoreType.REGULAR,
            pltpu.SemaphoreType.DMA((6,)),
            pltpu.SemaphoreType.DMA((8,)),
            pltpu.SemaphoreType.DMA((8,)),
            pltpu.SemaphoreType.DMA((8,)),
            pltpu.SemaphoreType.DMA((8,)),
            pltpu.SemaphoreType.DMA((4,)),
            pltpu.SemaphoreType.DMA((4,)),
            pltpu.SemaphoreType.DMA((2,)),
            pltpu.SemaphoreType.DMA((2,)),
            pltpu.SemaphoreType.DMA((2,)),
            pltpu.SemaphoreType.DMA((2,)),
            pltpu.SemaphoreType.DMA((128,)),
            pltpu.SemaphoreType.DMA((128,)),
            pltpu.SemaphoreType.DMA((128,)),
            pltpu.SemaphoreType.DMA((128,)),
        ],
        compiler_params=pltpu.CompilerParams(
            collective_id=1, has_side_effects=True, vmem_limit_bytes=62 * 2**20
        ),
        cost_estimate=pl.CostEstimate(
            flops=32_000_000_000, bytes_accessed=30_000_000, transcendentals=5_000_000
        ),
    )(
        q_in,
        kv_in,
        residual,
        out_proj,
        norm_gain.reshape(1, 4096),
        expert_ids,
        gate_weights,
        w_gate,
        w_up,
        w_down,
    )


def solution(mesh):
    in_specs = (
        P(("wide", "narrow"), None, None),
        P(("wide", "narrow"), None, None),
        P(("wide", "narrow"), None, None),
        P(("wide", "narrow"), None),
        P("narrow", None),
        P(),
        P(("wide", "narrow"), None),
        P(("wide", "narrow"), None),
        P(("wide", "narrow"), None, None),
        P(("wide", "narrow"), None, None),
        P(("wide", "narrow"), None, None),
    )
    out_specs = P(("wide", "narrow"), None)
    return jax.shard_map(shards, mesh=mesh, in_specs=in_specs, out_specs=out_specs, check_vma=False)
```

```python
import math

import jax
import jax.numpy as jnp
from jax import lax
from jax.experimental import pallas as pl
from jax.experimental.pallas import tpu as pltpu
from jax.sharding import PartitionSpec as P

MESH = pl.DeviceIdType.MESH
BF = jnp.bfloat16
F32 = jnp.float32


def offset_of(k):
    j = (128 - k) & 127
    return j, (j >> 2) + j, (j >> 4) + (j >> 2) + j, j >> 6


def peer_of(k, sign):
    wide, narrow = lax.axis_index("wide"), lax.axis_index("narrow")
    dx, dy, dz, dc = offset_of(k)
    x = ((wide >> 2) + sign * dx) & 3
    y = (wide + sign * dy) & 3
    z = ((narrow >> 1) + sign * dz) & 3
    c = (narrow + dc) & 1
    return (x * 4 + y, z * 2 + c)


def iota2(shape, dim):
    return lax.broadcasted_iota(jnp.int32, shape, dim)


def dot(a, b):
    return jnp.dot(a, b, preferred_element_type=F32)


def block_kernel(
    q_in,
    kv_in,
    res_hbm,
    proj_hbm,
    gain,
    ids,
    gates,
    wg_hbm,
    wu_hbm,
    wd_hbm,
    out,
    stage,
    recv,
    ret,
    wg,
    wu,
    wd,
    n2,
    g8,
    rows,
    inner,
    acc,
    q_all,
    kv_all,
    mixed,
    rank,
    rank_t,
    share_hi,
    share_lo,
    row_in,
    w_sem,
    q_send,
    q_recv,
    kv_send,
    kv_recv,
    s_send,
    s_recv,
    y_send,
    y_recv,
    l_send,
    l_recv,
    d_send,
    d_recv,
    r_send,
    r_recv,
):
    wide, narrow = lax.axis_index("wide"), lax.axis_index("narrow")
    z, c = narrow >> 1, narrow & 1

    def at(dz, dc):
        return ((z + dz) & 3) * 2 + ((c + dc) & 1)

    barrier = pltpu.get_barrier_semaphore()
    for d in range(1, 8):
        pl.semaphore_signal(
            barrier, inc=1, device_id=(wide, (narrow + d) & 7), device_id_type=MESH
        )
    for d in range(1, 16):
        pl.semaphore_signal(
            barrier, inc=1, device_id=((wide + d) & 15, narrow), device_id_type=MESH
        )

    proj = wd.at[0:512, :]
    load_proj = pltpu.make_async_copy(proj_hbm, proj, w_sem.at[0])
    load_proj.start()
    load_res = [
        pltpu.make_async_copy(
            res_hbm.at[:, h * 2048 : (h + 1) * 2048],
            n2.at[h * 128 : (h + 1) * 128, :],
            w_sem.at[1 + h],
        )
        for h in range(2)
    ]
    for load in load_res:
        load.start()

    def mine(start):
        return pl.ds(pl.multiple_of(start * 128, 128), 128)

    def send_q(s):
        to = at(s // 2, s % 2)
        return pltpu.make_async_remote_copy(
            src_ref=q_in.at[to],
            dst_ref=q_all.at[narrow],
            send_sem=q_send.at[s],
            recv_sem=q_recv.at[s],
            device_id=(wide, to),
            device_id_type=MESH,
        )

    def send_kv(s):
        to = at(s // 2, s % 2)
        return pltpu.make_async_remote_copy(
            src_ref=kv_in.at[to // 2],
            dst_ref=kv_all.at[:, mine(narrow), :],
            send_sem=kv_send.at[s],
            recv_sem=kv_recv.at[s],
            device_id=(wide, to),
            device_id_type=MESH,
        )

    own_q = pltpu.make_async_copy(q_in.at[narrow], q_all.at[narrow], q_recv.at[0])
    own_kv = pltpu.make_async_copy(kv_in.at[z], kv_all.at[:, mine(narrow), :], kv_recv.at[0])
    own_q.start()
    own_kv.start()
    pl.semaphore_wait(barrier, 22)
    for s in (4, 5, 2, 6, 3, 7, 1):
        send_kv(s).start()
    for s in (4, 5, 2, 6, 3, 7, 1):
        send_q(s).start()
    for d in range(1, 8):
        pl.semaphore_signal(row_in, inc=1, device_id=(wide, (narrow + d) & 7), device_id_type=MESH)

    loads = [
        pltpu.make_async_copy(src.at[0], dst, w_sem.at[3 + i])
        for i, (src, dst) in enumerate(((wg_hbm, wg), (wu_hbm, wu), (wd_hbm, wd)))
    ]
    loads[0].start()
    loads[1].start()

    def folded_at(ref, i, half=None):
        if half is None:
            return ref.at[i * 256 : (i + 1) * 256, 0:2048]
        return ref.at[i * 256 + half * 128 : i * 256 + (half + 1) * 128, 0:2048]

    def remote(src, dst, sends, recvs, i, to):
        return pltpu.make_async_remote_copy(
            src_ref=src,
            dst_ref=dst,
            send_sem=sends.at[i],
            recv_sem=recvs.at[i],
            device_id=(wide, to),
            device_id_type=MESH,
        )

    def to_sibling(i):
        return remote(folded_at(stage, 4 + i), folded_at(ret, i), s_send, s_recv, i, at(0, 1))

    def to_relay(i):
        return remote(
            folded_at(stage, 0, i), folded_at(ret, 6, i), y_send, y_recv, i, at((1, 3)[i], 0)
        )

    def to_owner(i):
        return remote(
            folded_at(stage, 1 + i), folded_at(ret, 4 + i), l_send, l_recv, i, at((1, 3)[i], 0)
        )

    wide_at, narrow_at = peer_of(iota2((128, 128), 0), 1)
    expert_at = wide_at * 8 + narrow_at
    chosen = jnp.zeros((128, 128), F32)
    share = jnp.zeros((128, 128), F32)
    for i in range(8):
        named = ids[i : i + 1, :] == expert_at
        chosen = jnp.where(named, 1.0, chosen)
        share = jnp.where(named, gates[i : i + 1, :], share)
    tri_row, tri_col = iota2((128, 128), 0), iota2((128, 128), 1)
    before = jnp.where(tri_row < tri_col, 1.0, 0.0).astype(BF)
    same = jnp.where(tri_row == tri_col, 1.0, 0.0).astype(BF)

    def turned(a):
        return lax.dot_general(same, a, (((1,), (1,)), ((), ())), preferred_element_type=F32)

    ranked = jnp.where(chosen > 0.5, dot(chosen.astype(BF), before), -1.0)
    rank_t[...] = ranked
    rank[...] = turned(ranked.astype(BF))
    share_hi[...] = turned(share.astype(BF)).astype(BF)
    share_lo[...] = turned((share - share.astype(BF).astype(F32)).astype(BF)).astype(BF)

    own_kv.wait()
    for s in range(1, 8):
        send_kv(s).wait_recv()
    load_proj.wait()

    scale = math.log2(math.e) / math.sqrt(128)
    q_row, k_col = iota2((256, 1024), 0) & 127, iota2((256, 1024), 1)

    def partial(i):
        dz = (2, 1, 3, 0)[i]
        back = (4 - dz) % 4
        for s in (back * 2, back * 2 + 1):
            if s == 0:
                own_q.wait()
            else:
                send_q(s).wait_recv()

        @pl.loop(0, 4)
        def _(step):
            block = at(dz, step // 2)
            part = pl.ds(pl.multiple_of((step % 2) * 256, 256), 256)
            query = q_all[block, part, :]
            scores = lax.dot_general(
                query, kv_all[0], (((1,), (1,)), ((), ())), preferred_element_type=F32
            )
            scores = jnp.where(q_row + block * 128 >= k_col, scores, -1e30)
            highest = jnp.max(scores, axis=-1, keepdims=True)
            weights = jnp.exp2((scores - highest) * scale)
            total = jnp.sum(weights, axis=-1, keepdims=True)
            both = (dot(weights.astype(BF), kv_all[1]) / total).astype(BF)
            down = mine(step // 2)
            mixed[down, pl.ds(pl.multiple_of((step % 2) * 256, 256), 128)] = both[0:128]
            mixed[down, pl.ds(pl.multiple_of((step % 2) * 256 + 128, 128), 128)] = both[128:256]

        @pl.loop(0, 4)
        def _(n):
            cols = pl.ds(pl.multiple_of(n * 1024, 1024), 1024)
            inside = pl.ds(pl.multiple_of((n % 2) * 1024, 1024), 1024)
            term = dot(mixed[...], wd[0:512, cols]).astype(BF)
            stage[pl.ds(pl.multiple_of(i * 256 + (n // 2) * 128, 128), 128), inside] = term[0:128]
            stage[pl.ds(pl.multiple_of(i * 256 + 1024 + (n // 2) * 128, 128), 128), inside] = term[
                128:256
            ]

        to_sibling(i).start()

    def pair(i, half):
        return folded_at(stage, i, half)[...].astype(F32) + folded_at(ret, i, half)[...].astype(F32)

    def passed_on(i):
        return folded_at(ret, 6, i)[...].astype(F32)

    partial(0)
    partial(1)
    to_sibling(0).wait_recv()
    for h in range(2):
        folded_at(stage, 0, h)[...] = pair(0, h).astype(BF)
        to_relay(h).start()
    partial(2)
    to_sibling(1).wait_recv()
    folded_at(stage, 1, 1)[...] = pair(1, 1).astype(BF)
    to_relay(0).wait_recv()
    folded_at(stage, 1, 0)[...] = (pair(1, 0) + passed_on(0)).astype(BF)
    to_owner(0).start()
    to_sibling(2).wait_recv()
    folded_at(stage, 2, 0)[...] = pair(2, 0).astype(BF)
    to_relay(1).wait_recv()
    folded_at(stage, 2, 1)[...] = (pair(2, 1) + passed_on(1)).astype(BF)
    to_owner(1).start()
    partial(3)
    loads[2].start()
    for load in load_res:
        load.wait()
    to_sibling(3).wait_recv()
    for h in range(2):
        half = slice(h * 128, (h + 1) * 128)
        acc[half, :] = n2[half, :].astype(F32) + pair(3, h)
    to_owner(0).wait_recv()
    to_owner(1).wait_recv()
    square = jnp.zeros((128, 1), F32)
    for h in range(2):
        half = slice(h * 128, (h + 1) * 128)
        full = acc[half, :] + (
            folded_at(ret, 4, h)[...].astype(F32) + folded_at(ret, 5, h)[...].astype(F32)
        )
        acc[half, :] = full
        square = square + jnp.sum(full * full, axis=-1, keepdims=True)
    factor = lax.rsqrt(square * (1.0 / 4096) + 1e-06)
    for h in range(2):
        half = slice(h * 128, (h + 1) * 128)
        n2[half, :] = (acc[half, :] * factor * gain[:, h * 2048 : (h + 1) * 2048]).astype(BF)

    for s in range(1, 8):
        send_kv(s).wait_send()
        send_q(s).wait_send()
    for i in range(4):
        to_sibling(i).wait_send()
    for i in range(2):
        to_relay(i).wait_send()
        to_owner(i).wait_send()

    to_row = iota2((256, 256), 0)
    to_col = iota2((256, 256), 1)

    def folded(i):
        return ((i >> 3) & 15) * 16 + (i >> 7) * 8 + (i & 7)

    def ones_where(mask):
        return jnp.where(mask, 1.0, 0.0).astype(BF)

    unfold = ones_where(to_col == folded(to_row))
    fold = ones_where(to_row == folded(to_col))
    swap = ones_where(to_col == (to_row & 15) * 16 + (to_row >> 4))

    def slab(k):
        return pl.ds(pl.multiple_of(k * 16, 16), 16)

    def group(q):
        return pl.ds(pl.multiple_of(q * 256, 256), 256)

    def dispatch(k):
        return pltpu.make_async_remote_copy(
            src_ref=stage.at[slab(k)],
            dst_ref=recv.at[slab(k)],
            send_sem=d_send.at[k],
            recv_sem=d_recv.at[k],
            device_id=peer_of(k, 1),
            device_id_type=MESH,
        )

    def give_back(k):
        return pltpu.make_async_remote_copy(
            src_ref=recv.at[slab(k)],
            dst_ref=ret.at[slab(k)],
            send_sem=r_send.at[k],
            recv_sem=r_recv.at[k],
            device_id=peer_of(k, -1),
            device_id_type=MESH,
        )

    own_in = pltpu.make_async_copy(stage.at[pl.ds(0, 16)], recv.at[pl.ds(0, 16)], d_recv.at[0])
    own_out = pltpu.make_async_copy(recv.at[pl.ds(0, 16)], ret.at[pl.ds(0, 16)], r_recv.at[0])

    pick8 = ones_where(rank_t[...] == 8.0)

    for n in range(4):
        half, inside = n // 2, slice((n % 2) * 1024, (n % 2 + 1) * 1024)
        g8[:, n * 1024 : (n + 1) * 1024] = dot(
            pick8, n2[half * 128 : (half + 1) * 128, inside]
        ).astype(BF)

    spread_row, spread_col = iota2((256, 128), 0), iota2((256, 128), 1)
    slot_row = (spread_row & 7).astype(F32)
    low_row = (spread_row & 8) == 0

    pl.semaphore_wait(row_in, 7)

    @pl.loop(0, 8)
    def _(q):
        spread = ones_where((spread_row >> 4) + q * 16 == spread_col)
        hit = dot(spread, rank_t[...].astype(BF)) == slot_row
        pick = jnp.concatenate(
            [ones_where(hit & low_row), ones_where(hit & jnp.logical_not(low_row))], axis=1
        )
        for n in range(4):
            stage[group(q), n * 512 : (n + 1) * 512] = dot(
                pick, n2[:, n * 512 : (n + 1) * 512]
            ).astype(BF)
        some = g8[slab(q), :]
        piled = jnp.concatenate([some[:, g * 256 : (g + 1) * 256] for g in range(16)], axis=0)
        stage[group(q), 2048:2304] = dot(swap, piled).astype(BF)

        @pl.loop(0, 16)
        def _(i):
            k = q * 16 + i

            @pl.when(k > 0)
            def _():
                dispatch(k).start()

    own_in.start()
    for load in loads:
        load.wait()

    @pl.loop(0, 4)
    def _(j):
        @pl.loop(0, 32)
        def _(i):
            k = j * 32 + i

            @pl.when(k > 0)
            def _():
                dispatch(k).wait_recv()

            @pl.when(k == 0)
            def _():
                own_in.wait()

        for q in range(2):
            part = group(j * 2 + q)
            for n in range(4):
                cols = slice(n * 512, (n + 1) * 512)
                wide_rows = dot(unfold, recv[part, cols]).astype(BF)
                rows[q * 128 : (q + 1) * 128, n * 512 : (n + 1) * 512] = wide_rows[0:128]
                rows[q * 128 : (q + 1) * 128, 2048 + n * 512 : 2048 + (n + 1) * 512] = wide_rows[
                    128:256
                ]
            last = dot(swap, recv[part, 2048:2304]).astype(BF)
            for g in range(16):
                rows[256 + q * 16 : 272 + q * 16, g * 256 : (g + 1) * 256] = last[
                    g * 16 : (g + 1) * 16
                ]

        @pl.loop(0, 3)
        def _(n):
            cols = pl.ds(pl.multiple_of(n * 256, 256), 256)
            gated = dot(rows[...], wg[:, cols])
            upward = dot(rows[...], wu[:, cols])
            inner[:, cols] = (gated / (1.0 + jnp.exp(-gated)) * upward).astype(BF)

        @pl.loop(0, 8)
        def _(n):
            cols = pl.ds(pl.multiple_of(n * 512, 512), 512)
            rows[:, cols] = dot(inner[...], wd[:, cols]).astype(BF)

        for q in range(2):
            part = group(j * 2 + q)
            for n in range(4):
                piled = jnp.concatenate(
                    [
                        rows[q * 128 : (q + 1) * 128, n * 512 : (n + 1) * 512],
                        rows[q * 128 : (q + 1) * 128, 2048 + n * 512 : 2048 + (n + 1) * 512],
                    ],
                    axis=0,
                )
                recv[part, n * 512 : (n + 1) * 512] = dot(fold, piled).astype(BF)
            piled = jnp.concatenate(
                [
                    rows[256 + q * 16 : 272 + q * 16, g * 256 : (g + 1) * 256]
                    for g in range(16)
                ],
                axis=0,
            )
            recv[part, 2048:2304] = dot(swap, piled).astype(BF)

        @pl.loop(0, 32)
        def _(i):
            k = j * 32 + i

            @pl.when(k > 0)
            def _():
                give_back(k).start()

            @pl.when(k == 0)
            def _():
                own_out.start()

    lane_row, lane_col = iota2((128, 256), 0), iota2((128, 256), 1)
    slot_col = (lane_col & 7).astype(F32)
    low_col = (lane_col & 8) == 0

    @pl.loop(0, 8)
    def _(q):
        @pl.loop(0, 16)
        def _(i):
            k = q * 16 + i

            @pl.when(k > 0)
            def _():
                give_back(k).wait_recv()

            @pl.when(k == 0)
            def _():
                own_out.wait()

        spread = ones_where((lane_col >> 4) + q * 16 == lane_row)
        hit = dot(rank[...].astype(BF), spread) == slot_col
        high = jnp.where(hit, dot(share_hi[...], spread), 0.0)
        low = jnp.where(hit, dot(share_lo[...], spread), 0.0)

        def both(a):
            return jnp.concatenate(
                [jnp.where(low_col, a, 0.0), jnp.where(low_col, 0.0, a)], axis=0
            ).astype(BF)

        mix_hi, mix_lo = both(high), both(low)
        for n in range(4):
            cols = slice(n * 512, (n + 1) * 512)
            block = ret[group(q), cols]
            acc[:, cols] += dot(mix_hi, block) + dot(mix_lo, block)
        last = dot(swap, ret[group(q), 2048:2304]).astype(BF)
        for g in range(16):
            g8[slab(q), g * 256 : (g + 1) * 256] = last[g * 16 : (g + 1) * 16]

    at_last = rank[...] == 8.0
    mix8_hi = jnp.where(at_last, share_hi[...].astype(F32), 0.0).astype(BF)
    mix8_lo = jnp.where(at_last, share_lo[...].astype(F32), 0.0).astype(BF)
    for n in range(8):
        cols = slice(n * 512, (n + 1) * 512)
        half, inside = n // 4, slice((n % 4) * 512, (n % 4 + 1) * 512)
        block = g8[:, cols]
        total = acc[half * 128 : (half + 1) * 128, inside]
        total = total + dot(mix8_hi, block) + dot(mix8_lo, block)
        out[:, cols] = total.astype(BF)

    @pl.loop(1, 128)
    def _(k):
        dispatch(k).wait_send()
        give_back(k).wait_send()


def shards(
    queries,
    keys,
    values,
    residual,
    out_proj,
    norm_gain,
    expert_ids,
    gate_weights,
    w_gate,
    w_up,
    w_down,
):
    q_in = jnp.transpose(queries, (1, 0, 2)).reshape(8, 512, 128)
    kv_in = jnp.transpose(jnp.stack([keys, values]), (2, 0, 1, 3))
    vmem = pl.BlockSpec(memory_space=pltpu.VMEM)
    hbm = pl.BlockSpec(memory_space=pl.ANY)
    return pl.pallas_call(
        block_kernel,
        out_shape=jax.ShapeDtypeStruct((128, 4096), BF),
        in_specs=[hbm] * 4 + [vmem] * 3 + [hbm] * 3,
        out_specs=vmem,
        scratch_shapes=[
            pltpu.VMEM((2048, 2304), BF),
            pltpu.VMEM((2048, 2304), BF),
            pltpu.VMEM((2048, 2304), BF),
            pltpu.VMEM((4096, 768), BF),
            pltpu.VMEM((4096, 768), BF),
            pltpu.VMEM((768, 4096), BF),
            pltpu.VMEM((256, 2048), BF),
            pltpu.VMEM((128, 4096), BF),
            pltpu.VMEM((288, 4096), BF),
            pltpu.VMEM((288, 768), BF),
            pltpu.VMEM((256, 2048), F32),
            pltpu.VMEM((8, 512, 128), BF),
            pltpu.VMEM((2, 1024, 128), BF),
            pltpu.VMEM((256, 512), BF),
            pltpu.VMEM((128, 128), F32),
            pltpu.VMEM((128, 128), F32),
            pltpu.VMEM((128, 128), BF),
            pltpu.VMEM((128, 128), BF),
            pltpu.SemaphoreType.REGULAR,
            pltpu.SemaphoreType.DMA((6,)),
            pltpu.SemaphoreType.DMA((8,)),
            pltpu.SemaphoreType.DMA((8,)),
            pltpu.SemaphoreType.DMA((8,)),
            pltpu.SemaphoreType.DMA((8,)),
            pltpu.SemaphoreType.DMA((4,)),
            pltpu.SemaphoreType.DMA((4,)),
            pltpu.SemaphoreType.DMA((2,)),
            pltpu.SemaphoreType.DMA((2,)),
            pltpu.SemaphoreType.DMA((2,)),
            pltpu.SemaphoreType.DMA((2,)),
            pltpu.SemaphoreType.DMA((128,)),
            pltpu.SemaphoreType.DMA((128,)),
            pltpu.SemaphoreType.DMA((128,)),
            pltpu.SemaphoreType.DMA((128,)),
        ],
        compiler_params=pltpu.CompilerParams(
            collective_id=1, has_side_effects=True, vmem_limit_bytes=62 * 2**20
        ),
        cost_estimate=pl.CostEstimate(
            flops=32_000_000_000, bytes_accessed=30_000_000, transcendentals=5_000_000
        ),
    )(
        q_in,
        kv_in,
        residual,
        out_proj,
        norm_gain.reshape(1, 4096),
        expert_ids.T,
        gate_weights.T,
        w_gate,
        w_up,
        w_down,
    )


def solution(mesh):
    in_specs = (
        P(("wide", "narrow"), None, None),
        P(("wide", "narrow"), None, None),
        P(("wide", "narrow"), None, None),
        P(("wide", "narrow"), None),
        P("narrow", None),
        P(),
        P(("wide", "narrow"), None),
        P(("wide", "narrow"), None),
        P(("wide", "narrow"), None, None),
        P(("wide", "narrow"), None, None),
        P(("wide", "narrow"), None, None),
    )
    out_specs = P(("wide", "narrow"), None)
    return jax.shard_map(shards, mesh=mesh, in_specs=in_specs, out_specs=out_specs, check_vma=False)
```

```python
import math

import jax
import jax.numpy as jnp
from jax import lax
from jax.experimental import pallas as pl
from jax.experimental.pallas import tpu as pltpu
from jax.sharding import PartitionSpec as P

MESH = pl.DeviceIdType.MESH
BF = jnp.bfloat16
F32 = jnp.float32


def offset_of(k):
    j = (128 - k) & 127
    return j, (j >> 2) + 2 * j, (j >> 4) + (j >> 2) + j, j >> 6


def peer_of(k, sign):
    wide, narrow = lax.axis_index("wide"), lax.axis_index("narrow")
    dx, dy, dz, dc = offset_of(k)
    x = ((wide >> 2) + sign * dx) & 3
    y = (wide + sign * dy) & 3
    z = ((narrow >> 1) + sign * dz) & 3
    c = (narrow + dc) & 1
    return (x * 4 + y, z * 2 + c)


def iota2(shape, dim):
    return lax.broadcasted_iota(jnp.int32, shape, dim)


def dot(a, b):
    return jnp.dot(a, b, preferred_element_type=F32)


def block_kernel(
    q_in,
    kv_in,
    res_hbm,
    proj_hbm,
    gain,
    ids,
    gates,
    wg_hbm,
    wu_hbm,
    wd_hbm,
    out,
    stage,
    recv,
    ret,
    wg,
    wu,
    wd,
    n2,
    g8,
    rows,
    inner,
    acc,
    q_all,
    kv_all,
    mixed,
    rank,
    rank_t,
    share_hi,
    share_lo,
    row_in,
    w_sem,
    q_send,
    q_recv,
    kv_send,
    kv_recv,
    s_send,
    s_recv,
    y_send,
    y_recv,
    l_send,
    l_recv,
    d_send,
    d_recv,
    r_send,
    r_recv,
):
    wide, narrow = lax.axis_index("wide"), lax.axis_index("narrow")
    z, c = narrow >> 1, narrow & 1

    def at(dz, dc):
        return ((z + dz) & 3) * 2 + ((c + dc) & 1)

    barrier = pltpu.get_barrier_semaphore()
    for d in range(1, 8):
        pl.semaphore_signal(
            barrier, inc=1, device_id=(wide, (narrow + d) & 7), device_id_type=MESH
        )
    for d in range(1, 16):
        pl.semaphore_signal(
            barrier, inc=1, device_id=((wide + d) & 15, narrow), device_id_type=MESH
        )

    proj = wd.at[0:512, :]
    load_proj = pltpu.make_async_copy(proj_hbm, proj, w_sem.at[0])
    load_proj.start()
    load_res = [
        pltpu.make_async_copy(
            res_hbm.at[:, h * 2048 : (h + 1) * 2048],
            n2.at[h * 128 : (h + 1) * 128, :],
            w_sem.at[1 + h],
        )
        for h in range(2)
    ]
    for load in load_res:
        load.start()

    def mine(start):
        return pl.ds(pl.multiple_of(start * 128, 128), 128)

    def send_q(s):
        to = at(s // 2, s % 2)
        return pltpu.make_async_remote_copy(
            src_ref=q_in.at[to],
            dst_ref=q_all.at[narrow],
            send_sem=q_send.at[s],
            recv_sem=q_recv.at[s],
            device_id=(wide, to),
            device_id_type=MESH,
        )

    def send_kv(s):
        to = at(s // 2, s % 2)
        return pltpu.make_async_remote_copy(
            src_ref=kv_in.at[to // 2],
            dst_ref=kv_all.at[:, mine(narrow), :],
            send_sem=kv_send.at[s],
            recv_sem=kv_recv.at[s],
            device_id=(wide, to),
            device_id_type=MESH,
        )

    own_q = pltpu.make_async_copy(q_in.at[narrow], q_all.at[narrow], q_recv.at[0])
    own_kv = pltpu.make_async_copy(kv_in.at[z], kv_all.at[:, mine(narrow), :], kv_recv.at[0])
    own_q.start()
    own_kv.start()
    pl.semaphore_wait(barrier, 22)
    for s in (4, 5, 2, 6, 3, 7, 1):
        send_kv(s).start()
    for s in (4, 5, 2, 6, 3, 7, 1):
        send_q(s).start()
    for d in range(1, 8):
        pl.semaphore_signal(row_in, inc=1, device_id=(wide, (narrow + d) & 7), device_id_type=MESH)

    loads = [
        pltpu.make_async_copy(src.at[0], dst, w_sem.at[3 + i])
        for i, (src, dst) in enumerate(((wg_hbm, wg), (wu_hbm, wu), (wd_hbm, wd)))
    ]
    loads[0].start()
    loads[1].start()

    def folded_at(ref, i, half=None):
        if half is None:
            return ref.at[i * 256 : (i + 1) * 256, 0:2048]
        return ref.at[i * 256 + half * 128 : i * 256 + (half + 1) * 128, 0:2048]

    def remote(src, dst, sends, recvs, i, to):
        return pltpu.make_async_remote_copy(
            src_ref=src,
            dst_ref=dst,
            send_sem=sends.at[i],
            recv_sem=recvs.at[i],
            device_id=(wide, to),
            device_id_type=MESH,
        )

    def to_sibling(i):
        return remote(folded_at(stage, 4 + i), folded_at(ret, i), s_send, s_recv, i, at(0, 1))

    def to_relay(i):
        return remote(
            folded_at(stage, 0, i), folded_at(ret, 6, i), y_send, y_recv, i, at((1, 3)[i], 0)
        )

    def to_owner(i):
        return remote(
            folded_at(stage, 1 + i), folded_at(ret, 4 + i), l_send, l_recv, i, at((1, 3)[i], 0)
        )

    wide_at, narrow_at = peer_of(iota2((128, 128), 0), 1)
    expert_at = wide_at * 8 + narrow_at
    chosen = jnp.zeros((128, 128), F32)
    share = jnp.zeros((128, 128), F32)
    for i in range(8):
        named = ids[i : i + 1, :] == expert_at
        chosen = jnp.where(named, 1.0, chosen)
        share = jnp.where(named, gates[i : i + 1, :], share)
    tri_row, tri_col = iota2((128, 128), 0), iota2((128, 128), 1)
    before = jnp.where(tri_row < tri_col, 1.0, 0.0).astype(BF)
    same = jnp.where(tri_row == tri_col, 1.0, 0.0).astype(BF)

    def turned(a):
        return lax.dot_general(same, a, (((1,), (1,)), ((), ())), preferred_element_type=F32)

    ranked = jnp.where(chosen > 0.5, dot(chosen.astype(BF), before), -1.0)
    rank_t[...] = ranked
    rank[...] = turned(ranked.astype(BF))
    share_hi[...] = turned(share.astype(BF)).astype(BF)
    share_lo[...] = turned((share - share.astype(BF).astype(F32)).astype(BF)).astype(BF)

    own_kv.wait()
    for s in range(1, 8):
        send_kv(s).wait_recv()
    load_proj.wait()

    scale = math.log2(math.e) / math.sqrt(128)
    q_row, k_col = iota2((256, 1024), 0) & 127, iota2((256, 1024), 1)

    def partial(i):
        dz = (2, 1, 3, 0)[i]
        back = (4 - dz) % 4
        for s in (back * 2, back * 2 + 1):
            if s == 0:
                own_q.wait()
            else:
                send_q(s).wait_recv()

        @pl.loop(0, 4)
        def _(step):
            block = at(dz, step // 2)
            part = pl.ds(pl.multiple_of((step % 2) * 256, 256), 256)
            query = q_all[block, part, :]
            scores = lax.dot_general(
                query, kv_all[0], (((1,), (1,)), ((), ())), preferred_element_type=F32
            )
            scores = jnp.where(q_row + block * 128 >= k_col, scores, -1e30)
            highest = jnp.max(scores, axis=-1, keepdims=True)
            weights = jnp.exp2((scores - highest) * scale)
            total = jnp.sum(weights, axis=-1, keepdims=True)
            both = (dot(weights.astype(BF), kv_all[1]) / total).astype(BF)
            down = mine(step // 2)
            mixed[down, pl.ds(pl.multiple_of((step % 2) * 256, 256), 128)] = both[0:128]
            mixed[down, pl.ds(pl.multiple_of((step % 2) * 256 + 128, 128), 128)] = both[128:256]

        @pl.loop(0, 4)
        def _(n):
            cols = pl.ds(pl.multiple_of(n * 1024, 1024), 1024)
            inside = pl.ds(pl.multiple_of((n % 2) * 1024, 1024), 1024)
            term = dot(mixed[...], wd[0:512, cols]).astype(BF)
            stage[pl.ds(pl.multiple_of(i * 256 + (n // 2) * 128, 128), 128), inside] = term[0:128]
            stage[pl.ds(pl.multiple_of(i * 256 + 1024 + (n // 2) * 128, 128), 128), inside] = term[
                128:256
            ]

        to_sibling(i).start()

    def pair(i, half):
        return folded_at(stage, i, half)[...].astype(F32) + folded_at(ret, i, half)[...].astype(F32)

    def passed_on(i):
        return folded_at(ret, 6, i)[...].astype(F32)

    partial(0)
    partial(1)
    to_sibling(0).wait_recv()
    for h in range(2):
        folded_at(stage, 0, h)[...] = pair(0, h).astype(BF)
        to_relay(h).start()
    partial(2)
    to_sibling(1).wait_recv()
    folded_at(stage, 1, 1)[...] = pair(1, 1).astype(BF)
    to_relay(0).wait_recv()
    folded_at(stage, 1, 0)[...] = (pair(1, 0) + passed_on(0)).astype(BF)
    to_owner(0).start()
    to_sibling(2).wait_recv()
    folded_at(stage, 2, 0)[...] = pair(2, 0).astype(BF)
    to_relay(1).wait_recv()
    folded_at(stage, 2, 1)[...] = (pair(2, 1) + passed_on(1)).astype(BF)
    to_owner(1).start()
    partial(3)
    loads[2].start()
    for load in load_res:
        load.wait()
    to_sibling(3).wait_recv()
    for h in range(2):
        half = slice(h * 128, (h + 1) * 128)
        acc[half, :] = n2[half, :].astype(F32) + pair(3, h)
    to_owner(0).wait_recv()
    to_owner(1).wait_recv()
    square = jnp.zeros((128, 1), F32)
    for h in range(2):
        half = slice(h * 128, (h + 1) * 128)
        full = acc[half, :] + (
            folded_at(ret, 4, h)[...].astype(F32) + folded_at(ret, 5, h)[...].astype(F32)
        )
        acc[half, :] = full
        square = square + jnp.sum(full * full, axis=-1, keepdims=True)
    factor = lax.rsqrt(square * (1.0 / 4096) + 1e-06)
    for h in range(2):
        half = slice(h * 128, (h + 1) * 128)
        n2[half, :] = (acc[half, :] * factor * gain[:, h * 2048 : (h + 1) * 2048]).astype(BF)

    for s in range(1, 8):
        send_kv(s).wait_send()
        send_q(s).wait_send()
    for i in range(4):
        to_sibling(i).wait_send()
    for i in range(2):
        to_relay(i).wait_send()
        to_owner(i).wait_send()

    to_row = iota2((256, 256), 0)
    to_col = iota2((256, 256), 1)

    def folded(i):
        return ((i >> 3) & 15) * 16 + (i >> 7) * 8 + (i & 7)

    def ones_where(mask):
        return jnp.where(mask, 1.0, 0.0).astype(BF)

    unfold = ones_where(to_col == folded(to_row))
    fold = ones_where(to_row == folded(to_col))
    swap = ones_where(to_col == (to_row & 15) * 16 + (to_row >> 4))

    def slab(k):
        return pl.ds(pl.multiple_of(k * 16, 16), 16)

    def group(q):
        return pl.ds(pl.multiple_of(q * 256, 256), 256)

    def dispatch(k):
        return pltpu.make_async_remote_copy(
            src_ref=stage.at[slab(k)],
            dst_ref=recv.at[slab(k)],
            send_sem=d_send.at[k],
            recv_sem=d_recv.at[k],
            device_id=peer_of(k, 1),
            device_id_type=MESH,
        )

    def give_back(k):
        return pltpu.make_async_remote_copy(
            src_ref=recv.at[slab(k)],
            dst_ref=ret.at[slab(k)],
            send_sem=r_send.at[k],
            recv_sem=r_recv.at[k],
            device_id=peer_of(k, -1),
            device_id_type=MESH,
        )

    own_in = pltpu.make_async_copy(stage.at[pl.ds(0, 16)], recv.at[pl.ds(0, 16)], d_recv.at[0])
    own_out = pltpu.make_async_copy(recv.at[pl.ds(0, 16)], ret.at[pl.ds(0, 16)], r_recv.at[0])

    pick8 = ones_where(rank_t[...] == 8.0)

    for n in range(4):
        half, inside = n // 2, slice((n % 2) * 1024, (n % 2 + 1) * 1024)
        g8[:, n * 1024 : (n + 1) * 1024] = dot(
            pick8, n2[half * 128 : (half + 1) * 128, inside]
        ).astype(BF)

    spread_row, spread_col = iota2((256, 128), 0), iota2((256, 128), 1)
    slot_row = (spread_row & 7).astype(F32)
    low_row = (spread_row & 8) == 0

    pl.semaphore_wait(row_in, 7)

    @pl.loop(0, 8)
    def _(q):
        spread = ones_where((spread_row >> 4) + q * 16 == spread_col)
        hit = dot(spread, rank_t[...].astype(BF)) == slot_row
        pick = jnp.concatenate(
            [ones_where(hit & low_row), ones_where(hit & jnp.logical_not(low_row))], axis=1
        )
        for n in range(4):
            stage[group(q), n * 512 : (n + 1) * 512] = dot(
                pick, n2[:, n * 512 : (n + 1) * 512]
            ).astype(BF)
        some = g8[slab(q), :]
        piled = jnp.concatenate([some[:, g * 256 : (g + 1) * 256] for g in range(16)], axis=0)
        stage[group(q), 2048:2304] = dot(swap, piled).astype(BF)

        @pl.loop(0, 16)
        def _(i):
            k = q * 16 + i

            @pl.when(k > 0)
            def _():
                dispatch(k).start()

    own_in.start()
    for load in loads:
        load.wait()

    @pl.loop(0, 4)
    def _(j):
        @pl.loop(0, 32)
        def _(i):
            k = j * 32 + i

            @pl.when(k > 0)
            def _():
                dispatch(k).wait_recv()

            @pl.when(k == 0)
            def _():
                own_in.wait()

        for q in range(2):
            part = group(j * 2 + q)
            for n in range(4):
                cols = slice(n * 512, (n + 1) * 512)
                wide_rows = dot(unfold, recv[part, cols]).astype(BF)
                rows[q * 128 : (q + 1) * 128, n * 512 : (n + 1) * 512] = wide_rows[0:128]
                rows[q * 128 : (q + 1) * 128, 2048 + n * 512 : 2048 + (n + 1) * 512] = wide_rows[
                    128:256
                ]
            last = dot(swap, recv[part, 2048:2304]).astype(BF)
            for g in range(16):
                rows[256 + q * 16 : 272 + q * 16, g * 256 : (g + 1) * 256] = last[
                    g * 16 : (g + 1) * 16
                ]

        @pl.loop(0, 3)
        def _(n):
            cols = pl.ds(pl.multiple_of(n * 256, 256), 256)
            gated = dot(rows[...], wg[:, cols])
            upward = dot(rows[...], wu[:, cols])
            inner[:, cols] = (gated / (1.0 + jnp.exp(-gated)) * upward).astype(BF)

        @pl.loop(0, 8)
        def _(n):
            cols = pl.ds(pl.multiple_of(n * 512, 512), 512)
            rows[:, cols] = dot(inner[...], wd[:, cols]).astype(BF)

        for q in range(2):
            part = group(j * 2 + q)
            for n in range(4):
                piled = jnp.concatenate(
                    [
                        rows[q * 128 : (q + 1) * 128, n * 512 : (n + 1) * 512],
                        rows[q * 128 : (q + 1) * 128, 2048 + n * 512 : 2048 + (n + 1) * 512],
                    ],
                    axis=0,
                )
                recv[part, n * 512 : (n + 1) * 512] = dot(fold, piled).astype(BF)
            piled = jnp.concatenate(
                [
                    rows[256 + q * 16 : 272 + q * 16, g * 256 : (g + 1) * 256]
                    for g in range(16)
                ],
                axis=0,
            )
            recv[part, 2048:2304] = dot(swap, piled).astype(BF)

        @pl.loop(0, 32)
        def _(i):
            k = j * 32 + i

            @pl.when(k > 0)
            def _():
                give_back(k).start()

            @pl.when(k == 0)
            def _():
                own_out.start()

    lane_row, lane_col = iota2((128, 256), 0), iota2((128, 256), 1)
    slot_col = (lane_col & 7).astype(F32)
    low_col = (lane_col & 8) == 0

    @pl.loop(0, 8)
    def _(q):
        @pl.loop(0, 16)
        def _(i):
            k = q * 16 + i

            @pl.when(k > 0)
            def _():
                give_back(k).wait_recv()

            @pl.when(k == 0)
            def _():
                own_out.wait()

        spread = ones_where((lane_col >> 4) + q * 16 == lane_row)
        hit = dot(rank[...].astype(BF), spread) == slot_col
        high = jnp.where(hit, dot(share_hi[...], spread), 0.0)
        low = jnp.where(hit, dot(share_lo[...], spread), 0.0)

        def both(a):
            return jnp.concatenate(
                [jnp.where(low_col, a, 0.0), jnp.where(low_col, 0.0, a)], axis=0
            ).astype(BF)

        mix_hi, mix_lo = both(high), both(low)
        for n in range(4):
            cols = slice(n * 512, (n + 1) * 512)
            block = ret[group(q), cols]
            acc[:, cols] += dot(mix_hi, block) + dot(mix_lo, block)
        last = dot(swap, ret[group(q), 2048:2304]).astype(BF)
        for g in range(16):
            g8[slab(q), g * 256 : (g + 1) * 256] = last[g * 16 : (g + 1) * 16]

    at_last = rank[...] == 8.0
    mix8_hi = jnp.where(at_last, share_hi[...].astype(F32), 0.0).astype(BF)
    mix8_lo = jnp.where(at_last, share_lo[...].astype(F32), 0.0).astype(BF)
    for n in range(8):
        cols = slice(n * 512, (n + 1) * 512)
        half, inside = n // 4, slice((n % 4) * 512, (n % 4 + 1) * 512)
        block = g8[:, cols]
        total = acc[half * 128 : (half + 1) * 128, inside]
        total = total + dot(mix8_hi, block) + dot(mix8_lo, block)
        out[:, cols] = total.astype(BF)

    @pl.loop(1, 128)
    def _(k):
        dispatch(k).wait_send()
        give_back(k).wait_send()


def shards(
    queries,
    keys,
    values,
    residual,
    out_proj,
    norm_gain,
    expert_ids,
    gate_weights,
    w_gate,
    w_up,
    w_down,
):
    q_in = jnp.transpose(queries, (1, 0, 2)).reshape(8, 512, 128)
    kv_in = jnp.transpose(jnp.stack([keys, values]), (2, 0, 1, 3))
    vmem = pl.BlockSpec(memory_space=pltpu.VMEM)
    hbm = pl.BlockSpec(memory_space=pl.ANY)
    return pl.pallas_call(
        block_kernel,
        out_shape=jax.ShapeDtypeStruct((128, 4096), BF),
        in_specs=[hbm] * 4 + [vmem] * 3 + [hbm] * 3,
        out_specs=vmem,
        scratch_shapes=[
            pltpu.VMEM((2048, 2304), BF),
            pltpu.VMEM((2048, 2304), BF),
            pltpu.VMEM((2048, 2304), BF),
            pltpu.VMEM((4096, 768), BF),
            pltpu.VMEM((4096, 768), BF),
            pltpu.VMEM((768, 4096), BF),
            pltpu.VMEM((256, 2048), BF),
            pltpu.VMEM((128, 4096), BF),
            pltpu.VMEM((288, 4096), BF),
            pltpu.VMEM((288, 768), BF),
            pltpu.VMEM((256, 2048), F32),
            pltpu.VMEM((8, 512, 128), BF),
            pltpu.VMEM((2, 1024, 128), BF),
            pltpu.VMEM((256, 512), BF),
            pltpu.VMEM((128, 128), F32),
            pltpu.VMEM((128, 128), F32),
            pltpu.VMEM((128, 128), BF),
            pltpu.VMEM((128, 128), BF),
            pltpu.SemaphoreType.REGULAR,
            pltpu.SemaphoreType.DMA((6,)),
            pltpu.SemaphoreType.DMA((8,)),
            pltpu.SemaphoreType.DMA((8,)),
            pltpu.SemaphoreType.DMA((8,)),
            pltpu.SemaphoreType.DMA((8,)),
            pltpu.SemaphoreType.DMA((4,)),
            pltpu.SemaphoreType.DMA((4,)),
            pltpu.SemaphoreType.DMA((2,)),
            pltpu.SemaphoreType.DMA((2,)),
            pltpu.SemaphoreType.DMA((2,)),
            pltpu.SemaphoreType.DMA((2,)),
            pltpu.SemaphoreType.DMA((128,)),
            pltpu.SemaphoreType.DMA((128,)),
            pltpu.SemaphoreType.DMA((128,)),
            pltpu.SemaphoreType.DMA((128,)),
        ],
        compiler_params=pltpu.CompilerParams(
            collective_id=1, has_side_effects=True, vmem_limit_bytes=62 * 2**20
        ),
        cost_estimate=pl.CostEstimate(
            flops=32_000_000_000, bytes_accessed=30_000_000, transcendentals=5_000_000
        ),
    )(
        q_in,
        kv_in,
        residual,
        out_proj,
        norm_gain.reshape(1, 4096),
        expert_ids.T,
        gate_weights.T,
        w_gate,
        w_up,
        w_down,
    )


def solution(mesh):
    in_specs = (
        P(("wide", "narrow"), None, None),
        P(("wide", "narrow"), None, None),
        P(("wide", "narrow"), None, None),
        P(("wide", "narrow"), None),
        P("narrow", None),
        P(),
        P(("wide", "narrow"), None),
        P(("wide", "narrow"), None),
        P(("wide", "narrow"), None, None),
        P(("wide", "narrow"), None, None),
        P(("wide", "narrow"), None, None),
    )
    out_specs = P(("wide", "narrow"), None)
    return jax.shard_map(shards, mesh=mesh, in_specs=in_specs, out_specs=out_specs, check_vma=False)
```
